128 devices in a mesh: slab: 32 (over z, y, x_hi), rxn: 4 (over x_lo, core).
Axes of the slice: x: 4 (x_hi: 2, x_lo: 2; x = x_hi * 2 + x_lo), y: 4, z: 4, core: 2. Of those that a mesh axis runs over, the one named last changes fastest.
Arguments:
- conc: float32 [256, 64, 4096], P('rxn', 'slab'), may hold values from 0.5 to 4
- order: int32 [2048, 256], P('rxn'), may hold values from 0 to 2, as said below
- stoich: int32 [256, 2048], P(None, 'rxn'), may hold values from -2 to 2, as said below
- species_class: int32 [256], P('rxn'), may hold values from 0 to 3
- diff_coef: float32 [4], replicated, may hold values from 0.1 to 1.5
- rate: float32 [2048], P('rxn'), may hold values from 0.05 to 1
- noise_load: float32 [2, 2048, 32], P(None, 'rxn'), may hold values from -6 to 6
- cell_noise: float32 [2, 32, 64, 4096], P(None, None, 'slab'), may hold values from -6 to 6
Outputs:
- final_conc: float32 [256, 64, 4096], P('rxn', 'slab')
The draws below stay inside these ranges and needn't reach their ends.
Inputs may be any that keep to these rules, and one draw needn't show every extreme that they name: `order`: each reaction has one or two reactant picks among the species; its row sums to 1 or 2. `stoich`: each column is minus the reaction's reactant orders plus two product picks.
All inputs are finite; a program needn't handle non-finite values.
Results may differ from the reference program's by a relative error of at most 0.0045.
Values may be sent and summed in bfloat16 or wider, within the bound.
No kernel may reach another device: no remote copies, remote signals or barrier semaphores. Data moves between devices by JAX's collectives and lax.ppermute only.
A program may use at most 192 MiB of HBM per device.

```python
import math
import jax
import jax.numpy as jnp
from jax import lax

S = 256
R = 2048
GX = 64
GY = 64
K = 32
STEPS = 2
NCLASS = 4
NZ = 64


def network_tables(key):
    keys = jax.random.split(key, 5)
    first = jax.random.randint(keys[0], (R,), 0, S)
    second = jax.random.randint(keys[1], (R,), 0, S)
    use_two = jax.random.randint(keys[2], (R,), 0, 2)
    made_one = jax.random.randint(keys[3], (R,), 0, S)
    made_two = jax.random.randint(keys[4], (R,), 0, S)
    ids = jnp.arange(S)[None, :]
    reactants = (first[:, None] == ids).astype(jnp.int32) + use_two[:, None] * (second[:, None] == ids).astype(jnp.int32)
    products = (made_one[:, None] == ids).astype(jnp.int32) + (made_two[:, None] == ids).astype(jnp.int32)
    return (reactants, products)


def draw_order(key, part):
    reactants, products = network_tables(key)
    return reactants.astype(jnp.int32)


def draw_stoich(key, part):
    reactants, products = network_tables(key)
    return jnp.transpose(products - reactants).astype(jnp.int32)


def with_ends(entries, own_key, smallest, largest):
    longest = entries.shape.index(max(entries.shape))
    spots = []
    for shift in (0, 1):
        where = [jax.random.randint(jax.random.fold_in(own_key, axis), (), 0, length) for axis, length in enumerate(entries.shape)]
        where[longest] = (where[longest] + shift) % entries.shape[longest]
        spots.append(tuple(where))
    return entries.at[spots[0]].set(smallest).at[spots[1]].set(largest)


def steps_of(key, extent, cuts, low, largest):
    def one(dim, blocks):
        steps = jax.random.uniform(jax.random.fold_in(jax.random.fold_in(key, 6), dim), (blocks,), jnp.float32, low / len(cuts), largest / len(cuts))
        return jnp.repeat(jnp.exp(steps), extent[dim] // blocks).reshape((-1,) + (1,) * (len(extent) - dim - 1))

    loudness = one(*cuts[0])
    for cut in cuts[1:]:
        loudness = loudness * one(*cut)
    return loudness


def gaussian(rng, dims, scale, most, cuts=(), held_as=jnp.bfloat16):
    loudness = steps_of(rng, dims, cuts, -0.22, 0.18) if cuts else 1.0
    drawn = jax.random.normal(rng, dims, jnp.float32) * scale * loudness
    return jnp.minimum(jnp.maximum(drawn, -most), most).astype(held_as)


def setup_inputs(seed: int = 0) -> dict:
    seeds = jax.random.split(jax.random.key(seed), 9)
    return {
        "conc": jnp.clip(jnp.exp(math.log(4.0) - 2.0794415 * jax.random.uniform(seeds[0], (S, NZ, GX * GY), jnp.float32) ** steps_of(seeds[0], (S, NZ, GX * GY), ((0, 4), (1, 32)), -0.2, 0.2)), 0.5, 4.0),
        "order": draw_order(jax.random.fold_in(seeds[8], 71), 0),
        "stoich": draw_stoich(jax.random.fold_in(seeds[8], 71), 0),
        "species_class": with_ends(jax.random.randint(seeds[3], (S,), 0, NCLASS), jax.random.fold_in(seeds[3], 1), 0, NCLASS - 1).astype(jnp.int32),
        "diff_coef": jnp.clip(jnp.exp(jax.random.uniform(seeds[4], (NCLASS,), jnp.float32, math.log(0.1), math.log(1.5))), 0.1, 1.5),
        "rate": jnp.clip(jnp.exp(math.log(1.0) - 2.9957323 * jax.random.uniform(seeds[5], (R,), jnp.float32) ** steps_of(seeds[5], (R,), ((0, 4),), -0.2, 0.2)), 0.05, 1.0),
        "noise_load": gaussian(seeds[6], (STEPS, R, K), 1.0, 6.0, ((1, 4),), jnp.float32),
        "cell_noise": gaussian(seeds[7], (STEPS, K, NZ, GX * GY), 1.0, 6.0, ((2, 32),), jnp.float32),
    }


tau_step = 0.1
floor_level = 0.02

def lateral(field):
    plane = GX * GY
    up_x = jnp.concatenate([field[..., GY:], field[..., plane - GY:]], -1)
    down_x = jnp.concatenate([field[..., :GY], field[..., :plane - GY]], -1)
    column = jnp.arange(plane) % GY
    up_y = jnp.where(column == GY - 1, field, jnp.concatenate([field[..., 1:], field[..., plane - 1:]], -1))
    down_y = jnp.where(column == 0, field, jnp.concatenate([field[..., :1], field[..., :plane - 1]], -1))
    return up_x + down_x + up_y + down_y

def reference(conc, order, stoich, species_class, diff_coef, rate, noise_load, cell_noise):
    table = (species_class[:, None] == jnp.arange(NCLASS)[None, :]).astype(jnp.float32)
    coef = lax.optimization_barrier(jnp.sum(table * diff_coef[None, :], axis=1))
    order_b = order.astype(jnp.bfloat16)
    stoich_b = stoich.astype(jnp.bfloat16)
    for step in range(STEPS):
        padded = jnp.concatenate([conc[:, :1], conc, conc[:, NZ - 1:]], 1)
        lap = padded[:, 2:] + padded[:, :-2] + lateral(conc) - 6.0 * conc
        diffused = conc + tau_step * coef[:, None, None] * lap
        logc = jnp.log(conc).astype(jnp.bfloat16)
        loads = noise_load[step]
        factors = cell_noise[step]

        def plane_change(zed):
            levels = lax.dynamic_index_in_dim(logc, zed, 1, keepdims=False)
            expo = jnp.dot(order_b, levels, preferred_element_type=jnp.float32)
            prop = rate[:, None] * jnp.exp(expo)
            cellf = lax.dynamic_index_in_dim(factors, zed, 1, keepdims=False)
            noise = jnp.dot(loads, cellf, precision=lax.Precision.HIGHEST) * K ** (-0.5)
            scaled = prop * tau_step
            flux = (scaled + jnp.sqrt(scaled) * noise).astype(jnp.bfloat16)
            return jnp.dot(stoich_b, flux, preferred_element_type=jnp.float32)
        change = lax.map(plane_change, jnp.arange(NZ))
        change = jnp.transpose(change, (1, 0, 2))
        conc = jnp.maximum(diffused + change, floor_level)
    return conc
```

```python
import functools

import jax
import jax.numpy as jnp
from jax import lax
from jax.experimental import pallas as pl
from jax.experimental.pallas import tpu as pltpu
from jax.sharding import Mesh, PartitionSpec as P

GY = 64
K = 32
STEPS = 2
S = 256
TAU = 0.1
FLOOR = 0.02
HALF_LOG2E = 0.7213475204444817

RING = ("x_hi", "x_lo", "core")
N = 8
SB = 64
LN = 512
WROWS = 656

F32 = jnp.float32
BF16 = jnp.bfloat16
VMEM = pl.BlockSpec(memory_space=pltpu.VMEM)
SMEM = pl.BlockSpec(memory_space=pltpu.SMEM)


def split2(v):
    hi = v.astype(BF16)
    return hi, (v - hi.astype(F32)).astype(BF16)


def split3(v):
    hi = v.astype(BF16)
    rest = v - hi.astype(F32)
    mid = rest.astype(BF16)
    return hi, mid, (rest - mid.astype(F32)).astype(BF16)


def pack_weights(order_ref, stoich_ref, load_ref, rate_ref, class_ref, coef_ref, w0_ref, w1_ref):
    cls = class_ref[...]
    coef = jnp.zeros(cls.shape, F32)
    for c in range(coef_ref.shape[0]):
        coef = jnp.where(cls == c, coef_ref[c], coef)
    coef = coef * TAU
    lr = 0.5 * jnp.log2(rate_ref[...] * TAU)
    lr3 = [v.astype(F32) for v in split3(lr)]
    co3 = [v.astype(F32) for v in split3(coef)]
    for h, out in ((0, w0_ref), (1, w1_ref)):
        rs = slice(h * 256, h * 256 + 256)
        out[0:256, :] = order_ref[rs, :].astype(F32).astype(BF16)
        out[256:512, :] = stoich_ref[:, rs].astype(F32).astype(BF16)
        for t in range(STEPS):
            hi, lo = split2(load_ref[t, :, rs] * (K ** -0.5))
            out[512 + 64 * t:544 + 64 * t, :] = hi
            out[544 + 64 * t:576 + 64 * t, :] = lo
        tail = jnp.concatenate(
            [v[:, rs] for v in lr3] + co3 + [jnp.zeros((10, 256), F32)], axis=0
        )
        out[640:656, :] = tail.astype(BF16)


def weights_call(order, stoich, load_t, rate, cls, coef):
    w = jax.ShapeDtypeStruct((WROWS, 256), BF16)
    return pl.pallas_call(
        pack_weights,
        out_shape=(w, w),
        in_specs=[VMEM] * 5 + [SMEM],
        out_specs=(VMEM, VMEM),
        name="pack_weights",
    )(order, stoich, load_t, rate, cls, coef)


def pack_conc(info_ref, conc_ref, *outs):
    me = info_ref[0]
    for k in range(N):
        lanes = pl.ds(pl.multiple_of((me ^ k) * LN, LN), LN)
        for p in range(2):
            outs[k][p] = conc_ref[:, p, lanes].astype(BF16)


def conc_call(info, conc):
    m = jax.ShapeDtypeStruct((2, SB, LN), BF16)
    return pl.pallas_call(
        pack_conc,
        out_shape=(m,) * N,
        in_specs=[SMEM, VMEM],
        out_specs=(VMEM,) * N,
        name="pack_conc",
    )(info, conc)


def pack_noise(info_ref, cell_ref, own_ref, far_ref):
    me = info_ref[0]
    for k, out in ((0, own_ref), (6, far_ref)):
        lanes = pl.ds(pl.multiple_of((me ^ k) * LN, LN), LN)
        for t in range(STEPS):
            for p in range(2):
                hi, lo = split2(cell_ref[t, :, p, lanes])
                out[t, p, 0:32] = hi
                out[t, p, 32:64] = lo


def noise_call(info, cell):
    m = jax.ShapeDtypeStruct((STEPS, 2, 2 * K, LN), BF16)
    return pl.pallas_call(
        pack_noise,
        out_shape=(m, m),
        in_specs=[SMEM, VMEM],
        out_specs=(VMEM, VMEM),
        name="pack_noise",
    )(info, cell)


def put_edges(plane_of, lo_ref, hi_ref, left_ref, right_ref):
    if lo_ref is not None:
        lo_ref[...] = plane_of(0).astype(BF16)
        hi_ref[...] = plane_of(3).astype(BF16)
    for q in range(2):
        a, b = plane_of(q).astype(F32), plane_of(q + 2).astype(F32)
        low = lax.broadcasted_iota(jnp.int32, (a.shape[0], 128), 1) < GY
        left_ref[q] = jnp.where(low, a[:, :128], pltpu.roll(b[:, :128], GY, 1)).astype(BF16)
        right_ref[q] = jnp.where(low, pltpu.roll(a[:, LN - 128:], GY, 1), b[:, LN - 128:]).astype(BF16)


def gather_conc(info_ref, *refs):
    pieces, (conc_ref, lo_ref, hi_ref, left_ref, right_ref) = refs[:N], refs[N:]
    me = info_ref[0]
    for k in range(N):
        src = me ^ k
        rows = pl.ds(pl.multiple_of((src & 3) * SB, SB), SB)
        for p in range(2):
            conc_ref[(src >> 2) * 2 + p, rows, :] = pieces[k][p]
    put_edges(lambda p: conc_ref[p], lo_ref, hi_ref, left_ref, right_ref)


EDGES = (
    jax.ShapeDtypeStruct((S, LN), BF16),
    jax.ShapeDtypeStruct((S, LN), BF16),
    jax.ShapeDtypeStruct((2, S, 128), BF16),
    jax.ShapeDtypeStruct((2, S, 128), BF16),
)


def gather_call(info, pieces):
    return pl.pallas_call(
        gather_conc,
        out_shape=(jax.ShapeDtypeStruct((4, S, LN), BF16),) + EDGES,
        in_specs=[SMEM] + [VMEM] * N,
        out_specs=(VMEM,) * 5,
        name="gather_conc",
    )(info, *pieces)


def react(step, info_ref, conc_ref, own_ref, far_ref, *refs):
    ws, refs = refs[:N], refs[N:]
    if step == 0:
        change_ref, coef_ref, load_s, lr_s, stoich_s, flux_s = refs
    else:
        change_ref, load_s, lr_s, stoich_s, flux_s = refs
        coef_ref = None
    me = info_ref[0]

    @pl.when(pl.program_id(0) == 0)
    def _():
        for i, w in enumerate(ws):
            rows = pl.ds(i * 256, 256)
            base = 512 + 64 * step
            hi, lo = w[base:base + 32, :].astype(F32), w[base + 32:base + 64, :].astype(F32)
            tail = w[640:656, :].astype(F32)
            block = jnp.concatenate([hi, hi, lo, tail, jnp.zeros((16, 256), F32)], axis=0)
            turned = block.T
            lane = lax.broadcasted_iota(jnp.int32, turned.shape, 1)
            load_s[rows, :] = jnp.where(lane < 96, turned, 0.0).astype(BF16)
            lr = turned[:, 96:97] + turned[:, 97:98] + turned[:, 98:99]
            lr_s[rows, :] = jnp.broadcast_to(lr, (256, 128))
            stoich_s[:, rows] = w[256:512, :]
            if coef_ref is not None and i % 2 == 0:
                co = turned[:SB, 99:100] + turned[:SB, 100:101] + turned[:SB, 101:102]
                at = pl.ds(pl.multiple_of(((me & 3) ^ (i // 2)) * SB, SB), SB)
                coef_ref[at, :] = jnp.broadcast_to(co, (SB, 128))

    logs = jnp.log(conc_ref[0].astype(F32)).astype(BF16)
    mine = (pl.program_id(0) // 2) == (me >> 2)
    p = pl.program_id(0) % 2
    cells = jnp.where(mine, own_ref[0, p].astype(F32), far_ref[0, p].astype(F32)).astype(BF16)
    cells = jnp.concatenate([cells, cells[:32], jnp.zeros((32, LN), BF16)], axis=0)
    for i, w in enumerate(ws):
        rows = pl.ds(i * 256, 256)
        expo = jnp.dot(w[0:256, :], logs, preferred_element_type=F32)
        noise = jnp.dot(load_s[rows, :], cells, preferred_element_type=F32)
        lr = lr_s[rows, :]
        root = jnp.exp2(expo * HALF_LOG2E + jnp.concatenate([lr] * (LN // 128), axis=1))
        flux_s[rows, :] = (root * (root + noise)).astype(BF16)
    change_ref[0] = jnp.dot(stoich_s[...], flux_s[...], preferred_element_type=F32)


def react_call(step, info, conc, own, far, ws):
    plane = pl.BlockSpec((1, S, LN), lambda p: (p, 0, 0))
    cell = pl.BlockSpec((1, 2, 2 * K, LN), lambda p: (step, 0, 0, 0))
    whole = pl.BlockSpec((WROWS, 256), lambda p: (0, 0))
    out_shape = [jax.ShapeDtypeStruct((4, S, LN), F32)]
    out_specs = [plane]
    if step == 0:
        out_shape.append(jax.ShapeDtypeStruct((S, 128), F32))
        out_specs.append(pl.BlockSpec((S, 128), lambda p: (0, 0)))
    return pl.pallas_call(
        functools.partial(react, step),
        grid=(4,),
        out_shape=out_shape,
        in_specs=[SMEM, plane, cell, cell] + [whole] * N,
        out_specs=out_specs,
        scratch_shapes=[
            pltpu.VMEM((2048, 128), BF16),
            pltpu.VMEM((2048, 128), F32),
            pltpu.VMEM((S, 2048), BF16),
            pltpu.VMEM((2048, LN), BF16),
        ],
        compiler_params=pltpu.CompilerParams(vmem_limit_bytes=40 << 20),
        cost_estimate=pl.CostEstimate(flops=13_000_000_000, bytes_accessed=8 << 20, transcendentals=5_000_000),
        name="react",
    )(info, conc, own, far, *ws)


def diffuse_planes(info_ref, state, lo, hi, left, right, change, coef):
    me = info_ref[0]
    ring = info_ref[1]
    planes = [state(p).astype(F32) for p in range(4)]
    rows = planes[0].shape[0]
    lane = lax.broadcasted_iota(jnp.int32, (rows, 128), 1)
    low = lane < GY
    column = lane % GY
    at_start = (me == 0).astype(jnp.int32)
    at_end = (me == N - 1).astype(jnp.int32)
    below = jnp.where(ring == 0, planes[0], lo.astype(F32))
    above = jnp.where(ring == 15, planes[3], hi.astype(F32))
    out = []
    for p in range(4):
        c = planes[p]
        dn = below if p == 0 else planes[p - 1]
        up = above if p == 3 else planes[p + 1]
        lef = left(p % 2).astype(F32)
        rig = right(p % 2).astype(F32)
        if p >= 2:
            lef = pltpu.roll(lef, GY, 1)
        else:
            rig = pltpu.roll(rig, GY, 1)
        vs = [c[:, 128 * j:128 * j + 128] for j in range(LN // 128)]
        sw = [pltpu.roll(v, GY, 1) for v in vs]
        lef = jnp.where(at_start == 1, vs[0], lef)
        rig = jnp.where(at_end == 1, vs[-1], rig)
        lat = []
        for j, v in enumerate(vs):
            prev = lef if j == 0 else sw[j - 1]
            nxt = rig if j == len(vs) - 1 else sw[j + 1]
            x_dn = jnp.where(low, prev, sw[j])
            x_up = jnp.where(low, sw[j], nxt)
            y_up = jnp.where(column == GY - 1, v, pltpu.roll(v, 127, 1))
            y_dn = jnp.where(column == 0, v, pltpu.roll(v, 1, 1))
            lat.append(x_up + x_dn + y_up + y_dn)
        lap = up + dn + jnp.concatenate(lat, axis=1) - 6.0 * c
        co = jnp.concatenate([coef] * (LN // 128), axis=1)
        out.append(jnp.maximum(c + co * lap + change(p), FLOOR))
    return out


def advance(info_ref, state_ref, change_ref, lo_ref, hi_ref, left_ref, right_ref, coef_ref, new_ref, *edges):
    new = diffuse_planes(
        info_ref, lambda p: state_ref[p], lo_ref[...], hi_ref[...], lambda q: left_ref[q], lambda q: right_ref[q],
        lambda p: change_ref[p], coef_ref[...],
    )
    for p in range(4):
        new_ref[p] = new[p].astype(new_ref.dtype)
    if edges:
        put_edges(lambda p: new[p], *edges)


ROWS = 64


def advance_call(info, state, change, halos, coef, last):
    four = pl.BlockSpec((4, ROWS, LN), lambda s: (0, s, 0))
    one = pl.BlockSpec((ROWS, LN), lambda s: (s, 0))
    side = pl.BlockSpec((2, ROWS, 128), lambda s: (0, s, 0))
    cof = pl.BlockSpec((ROWS, 128), lambda s: (s, 0))
    out_shape = [jax.ShapeDtypeStruct((4, S, LN), BF16 if last else F32)]
    out_specs = [four]
    if not last:
        out_shape += EDGES
        out_specs += [one, one, side, side]
    return pl.pallas_call(
        advance,
        grid=(S // ROWS,),
        out_shape=out_shape,
        in_specs=[SMEM, four, four, one, one, side, side, cof],
        out_specs=out_specs,
        compiler_params=pltpu.CompilerParams(vmem_limit_bytes=32 << 20),
        name="advance",
    )(info, state, change, *halos, coef)


def split_out(info_ref, state_ref, *outs):
    me = info_ref[0]
    for k in range(N):
        dst = me ^ k
        rows = pl.ds(pl.multiple_of((dst & 3) * SB, SB), SB)
        for p in range(2):
            outs[k][p] = state_ref[(dst >> 2) * 2 + p, rows, :]


def split_call(info, state):
    m = jax.ShapeDtypeStruct((2, SB, LN), BF16)
    return pl.pallas_call(
        split_out,
        out_shape=(m,) * N,
        in_specs=[SMEM, VMEM],
        out_specs=(VMEM,) * N,
        name="split_out",
    )(info, state)


def join_out(info_ref, *refs):
    pieces, out_ref = refs[:N], refs[N]
    me = info_ref[0]
    for k in range(N):
        lanes = pl.ds(pl.multiple_of((me ^ k) * LN, LN), LN)
        for p in range(2):
            out_ref[:, p, lanes] = pieces[k][p].astype(F32)


def join_call(info, pieces):
    return pl.pallas_call(
        join_out,
        out_shape=jax.ShapeDtypeStruct((SB, 2, N * LN), F32),
        in_specs=[SMEM] + [VMEM] * N,
        out_specs=VMEM,
        name="join_out",
    )(info, *pieces)


def send(v, k):
    return lax.ppermute(v, RING, [(i, i ^ k) for i in range(N)])


def halos(edges):
    lo, hi, left, right = edges
    up = [(r, r + 1) for r in range(15)]
    down = [(r + 1, r) for r in range(15)]
    from_below = lax.ppermute(hi, "zy", up)
    from_above = lax.ppermute(lo, "zy", down)
    from_left = lax.ppermute(right, RING, [(i, i + 1) for i in range(N - 1)])
    from_right = lax.ppermute(left, RING, [(i + 1, i) for i in range(N - 1)])
    return from_below, from_above, from_left, from_right


def on_device(conc, order, stoich, species_class, diff_coef, rate, noise_load, cell_noise):
    info = jnp.stack([lax.axis_index(RING), lax.axis_index("zy")]).astype(jnp.int32)
    w0, w1 = weights_call(
        order, stoich, jnp.transpose(noise_load, (0, 2, 1)), rate[None, :],
        jnp.pad(species_class, (0, 192))[None, :], diff_coef,
    )
    msgs = conc_call(info, conc)
    own, far = noise_call(info, cell_noise)
    far0, far1 = far, far
    rw0 = send(w0, 2)
    rw1 = send(w1, 6)
    pieces = [msgs[0]] + [send(msgs[k], k) for k in range(1, N)]
    far = send(far, 6)
    ws = [w0, w1, send(w0, 1), send(w1, 1), rw0, rw1, send(rw0, 1), send(rw1, 1)]
    state, *edges = gather_call(info, pieces)
    coef = None
    for step in range(STEPS):
        around = halos(edges)
        change, *more = react_call(step, info, state, own, far, ws)
        if more:
            coef = more[0]
        state, *edges = advance_call(info, state, change, around, coef, step == STEPS - 1)
    outs = split_call(info, state)
    back = [outs[0]] + [send(outs[k], k) for k in range(1, N)]
    return join_call(info, back)


def solution(mesh):
    grid = Mesh(mesh.devices.reshape(16, 2, 2, 2), ("zy", "x_hi", "x_lo", "core"))
    rxn, slab = ("x_lo", "core"), ("zy", "x_hi")
    placed = (
        P(rxn, slab, None),
        P(rxn, None),
        P(None, rxn),
        P(rxn),
        P(),
        P(rxn),
        P(None, rxn, None),
        P(None, None, slab, None),
    )
    return jax.shard_map(
        on_device, mesh=grid, in_specs=placed, out_specs=P(rxn, slab, None), check_vma=False
    )
```

```python
import functools

import jax
import jax.numpy as jnp
from jax import lax
from jax.experimental import pallas as pl
from jax.experimental.pallas import tpu as pltpu
from jax.sharding import Mesh, PartitionSpec as P

GY = 64
K = 32
STEPS = 2
S = 256
TAU = 0.1
FLOOR = 0.02
HALF_LOG2E = 0.7213475204444817

RING = ("x_hi", "x_lo", "core")
N = 8
SB = 64
LN = 512
FAR = 384
WROWS = 656

F32 = jnp.float32
BF16 = jnp.bfloat16
COST = pl.CostEstimate(flops=1, bytes_accessed=1, transcendentals=0)
VMEM = pl.BlockSpec(memory_space=pltpu.VMEM)
SMEM = pl.BlockSpec(memory_space=pltpu.SMEM)


def split2(v):
    hi = v.astype(BF16)
    return hi, (v - hi.astype(F32)).astype(BF16)


def split3(v):
    hi = v.astype(BF16)
    rest = v - hi.astype(F32)
    mid = rest.astype(BF16)
    return hi, mid, (rest - mid.astype(F32)).astype(BF16)


def pack_weights(order_ref, stoich_ref, load_ref, rate_ref, class_ref, coef_ref, w_ref):
    cls = class_ref[...]
    coef = jnp.zeros(cls.shape, F32)
    for c in range(coef_ref.shape[0]):
        coef = jnp.where(cls == c, coef_ref[c], coef)
    lr = 0.5 * jnp.log2(rate_ref[...] * TAU)
    lr3 = [v.astype(F32) for v in split3(lr)]
    co3 = [jnp.concatenate([v.astype(F32), jnp.zeros((1, 192), F32)], axis=1) for v in split3(coef * TAU)]
    for h in range(2):
        out = w_ref.at[h]
        rs = slice(h * 256, h * 256 + 256)
        out[0:256, :] = order_ref[rs, :].astype(F32).astype(BF16)
        out[256:512, :] = stoich_ref[:, rs].astype(F32).astype(BF16)
        for t in range(STEPS):
            hi, lo = split2(load_ref[t, :, rs] * (K ** -0.5))
            out[512 + 64 * t:544 + 64 * t, :] = hi
            out[544 + 64 * t:576 + 64 * t, :] = lo
        tail = jnp.concatenate([v[:, rs] for v in lr3] + co3 + [jnp.zeros((10, 256), F32)], axis=0)
        out[640:656, :] = tail.astype(BF16)


def params(mib):
    return pltpu.CompilerParams(vmem_limit_bytes=mib << 20)


def weights_call(order, stoich, load_t, rate, cls, coef):
    return pl.pallas_call(
        pack_weights,
        out_shape=jax.ShapeDtypeStruct((2, WROWS, 256), BF16),
        in_specs=[VMEM] * 5 + [SMEM],
        out_specs=VMEM,
        compiler_params=params(60),
        name="pack_weights",
        cost_estimate=COST,
    )(order, stoich, load_t, rate, cls, coef)


def pack_state(info_ref, conc_ref, cell_ref, self_ref, peer_ref, inner_ref, opp_ref, outer_ref, near_ref,
               buf, cells, sem, cell_sem):
    me = info_ref[0]
    order = (2, 3, 6, 7, 4, 5, 0, 1)
    places = {2: (inner_ref, 0), 3: (inner_ref, 2), 6: (outer_ref, 0), 7: (outer_ref, 2), 4: (opp_ref, 0),
              5: (opp_ref, 2), 0: (self_ref, 0), 1: (peer_ref, 0)}

    def lanes(k):
        return pl.ds(pl.multiple_of((me ^ k) * LN, LN), LN)

    copies = {}
    for k in order:
        for p in range(2):
            copies[k, p] = pltpu.make_async_copy(conc_ref.at[:, p, lanes(k)], buf.at[k, p], sem.at[k, p])
            copies[k, p].start()
    noise = {}
    for i, k in enumerate((6, 0)):
        for t in range(STEPS):
            for p in range(2):
                c = pltpu.make_async_copy(cell_ref.at[t, :, p, lanes(k)], cells.at[i, t, p], cell_sem.at[i, t, p])
                c.start()
                noise[i, t, p] = c
    for k in order:
        out, at = places[k]
        for p in range(2):
            copies[k, p].wait()
            out[SB * (at + p):SB * (at + p + 1)] = buf[k, p].astype(BF16)
    for t in range(STEPS):
        for p in range(2):
            for i in range(2):
                noise[i, t, p].wait()
            hi, lo = split2(cells[1, t, p])
            near_ref[t, p, 0:32] = hi
            near_ref[t, p, 32:64] = lo
            at = 4 * SB + 2 * K * t + K * p
            outer_ref[at:at + K] = cells[0, t, p].astype(BF16)


def state_call(info, conc, cell):
    def m(rows):
        return jax.ShapeDtypeStruct((rows, LN), BF16)

    any_ = pl.BlockSpec(memory_space=pl.ANY)
    return pl.pallas_call(
        pack_state,
        out_shape=(m(128), m(128), m(256), m(256), m(FAR), jax.ShapeDtypeStruct((STEPS, 2, SB, LN), BF16)),
        in_specs=[SMEM, any_, any_],
        out_specs=(VMEM,) * 6,
        scratch_shapes=[
            pltpu.VMEM((N, 2, SB, LN), F32),
            pltpu.VMEM((2, STEPS, 2, K, LN), F32),
            pltpu.SemaphoreType.DMA((N, 2)),
            pltpu.SemaphoreType.DMA((2, STEPS, 2)),
        ],
        compiler_params=params(60),
        name="pack_state",
        cost_estimate=COST,
    )(info, conc, cell)


PARTS = (0, 224, 448, WROWS)


def sort_weights(info_ref, *refs):
    own, beside, far, *parts = refs[:6]
    order_ref, stoich_ref, load_ref, lr_ref, coef_ref = refs[6:]
    me = info_ref[0]
    for i in range(N):
        def rows_of(start, stop, i=i):
            if i < 6:
                return (own, beside, far)[i // 2][i % 2, start:stop]
            cuts = [(max(start, lo) - lo, min(stop, hi) - lo) for lo, hi in zip(PARTS, PARTS[1:])]
            return jnp.concatenate([p[i % 2, lo:hi] for p, (lo, hi) in zip(parts, cuts) if lo < hi], axis=0)

        rows = pl.ds(i * 256, 256)
        order_ref[rows, :] = rows_of(0, 256)
        stoich_ref[:, rows] = rows_of(256, 512)
        loads = rows_of(512, WROWS).astype(F32)
        tail = loads[128:]
        for t in range(STEPS):
            hi, lo = loads[64 * t:64 * t + 32], loads[64 * t + 32:64 * t + 64]
            block = jnp.concatenate([hi, hi, lo, tail, jnp.zeros((16, 256), F32)], axis=0)
            turned = block.T
            lane = lax.broadcasted_iota(jnp.int32, turned.shape, 1)
            load_ref[t, rows, :] = jnp.where(lane < 96, turned, 0.0).astype(BF16)
        lr = turned[:, 96:97] + turned[:, 97:98] + turned[:, 98:99]
        lr_ref[rows, :] = jnp.broadcast_to(lr, (256, 128))
        if i % 2 == 0:
            co = turned[:SB, 99:100] + turned[:SB, 100:101] + turned[:SB, 101:102]
            at = pl.ds(pl.multiple_of(((me & 3) ^ (i // 2)) * SB, SB), SB)
            coef_ref[at, :] = jnp.broadcast_to(co, (SB, 128))


def sort_call(info, ws):
    return pl.pallas_call(
        sort_weights,
        out_shape=(
            jax.ShapeDtypeStruct((2048, S), BF16),
            jax.ShapeDtypeStruct((S, 2048), BF16),
            jax.ShapeDtypeStruct((STEPS, 2048, 128), BF16),
            jax.ShapeDtypeStruct((2048, 128), F32),
            jax.ShapeDtypeStruct((S, 128), F32),
        ),
        in_specs=[SMEM] + [VMEM] * 6,
        out_specs=(VMEM,) * 5,
        compiler_params=params(10),
        name="sort_weights",
        cost_estimate=COST,
    )(info, *ws)


def gather_planes(at, info_ref, *refs):
    pieces, out_ref = refs[:4], refs[4]
    me = info_ref[0]
    for j in range(4):
        rows = pl.ds(pl.multiple_of(((me & 3) ^ j) * SB, SB), SB)
        for p in range(2):
            out_ref[p, rows, :] = pieces[j][SB * (at[j] + p):SB * (at[j] + p + 1)]


def gather_call(info, pieces, at):
    return pl.pallas_call(
        functools.partial(gather_planes, at),
        out_shape=jax.ShapeDtypeStruct((2, S, LN), BF16),
        in_specs=[SMEM] + [VMEM] * 4,
        out_specs=VMEM,
        compiler_params=params(6),
        name="gather_planes",
        cost_estimate=COST,
    )(info, *pieces)


def put_edges(info_ref, a, b, ev_ref, od_ref, peer_ref, chip_ref):
    me = info_ref[0]
    first = (me >> 2) == 0
    core = me & 1
    even = (info_ref[1] & 1) == 0
    lo = jnp.where(first, a[0].astype(F32), b[0].astype(F32))
    hi = jnp.where(first, b[1].astype(F32), a[1].astype(F32))
    ev_ref[...] = jnp.where(even, hi, lo).astype(BF16)
    od_ref[...] = jnp.where(even, lo, hi).astype(BF16)
    for q in range(2):
        sides = []
        for cut in (slice(0, 128), slice(LN - 128, LN)):
            va, vb = a[q][:, cut].astype(F32), b[q][:, cut].astype(F32)
            sides.append((jnp.where(first, va, vb), jnp.where(first, vb, va)))
        low = lax.broadcasted_iota(jnp.int32, sides[0][0].shape, 1) < GY
        left = jnp.where(low, sides[0][0], pltpu.roll(sides[0][1], GY, 1))
        right = jnp.where(low, pltpu.roll(sides[1][0], GY, 1), sides[1][1])
        peer_ref[q] = jnp.where(core == 0, right, left).astype(BF16)
        chip_ref[q] = jnp.where(core == 0, left, right).astype(BF16)


EDGES = (
    jax.ShapeDtypeStruct((S, LN), BF16),
    jax.ShapeDtypeStruct((S, LN), BF16),
    jax.ShapeDtypeStruct((2, S, 128), BF16),
    jax.ShapeDtypeStruct((2, S, 128), BF16),
)


def edge_kernel(info_ref, a_ref, b_ref, *edges):
    put_edges(info_ref, [a_ref[0], a_ref[1]], [b_ref[0], b_ref[1]], *edges)


def edges_call(info, a, b):
    return pl.pallas_call(
        edge_kernel,
        out_shape=EDGES,
        in_specs=[SMEM, VMEM, VMEM],
        out_specs=(VMEM,) * 4,
        compiler_params=params(6),
        name="edges",
        cost_estimate=COST,
    )(info, a, b)


def react(far, conc_ref, cell_ref, order_ref, stoich_ref, load_ref, lr_ref, change_ref, flux_s):
    logs = jnp.log(conc_ref[0].astype(F32)).astype(BF16)
    zeros = jnp.zeros((K, LN), BF16)
    if far:
        hi, lo = cell_ref[...], zeros
    else:
        hi, lo = cell_ref[0, 0, :K], cell_ref[0, 0, K:]
    cells = jnp.concatenate([hi, lo, hi, zeros], axis=0)
    for i in range(N):
        rows = pl.ds(i * 256, 256)
        expo = jnp.dot(order_ref[rows, :], logs, preferred_element_type=F32)
        noise = jnp.dot(load_ref[0, rows, :], cells, preferred_element_type=F32)
        lr = lr_ref[rows, :]
        root = jnp.exp2(expo * HALF_LOG2E + jnp.concatenate([lr] * (LN // 128), axis=1))
        flux_s[rows, :] = (root * (root + noise)).astype(BF16)
    change_ref[0] = jnp.dot(stoich_ref[...], flux_s[...], preferred_element_type=F32)


def react_call(step, conc, cells, sorted_ws, far=False):
    order, stoich, load, lr, _ = sorted_ws
    plane = pl.BlockSpec((1, S, LN), lambda p: (p, 0, 0))
    if far:
        cell = pl.BlockSpec((K, LN), lambda p: (4 * SB // K + 2 * step + p, 0))
    else:
        cell = pl.BlockSpec((1, 1, 2 * K, LN), lambda p: (step, p, 0, 0))
    return pl.pallas_call(
        functools.partial(react, far),
        grid=(2,),
        out_shape=jax.ShapeDtypeStruct((2, S, LN), F32),
        in_specs=[
            plane,
            cell,
            pl.BlockSpec((2048, S), lambda p: (0, 0)),
            pl.BlockSpec((S, 2048), lambda p: (0, 0)),
            pl.BlockSpec((1, 2048, 128), lambda p: (step, 0, 0)),
            pl.BlockSpec((2048, 128), lambda p: (0, 0)),
        ],
        out_specs=plane,
        scratch_shapes=[pltpu.VMEM((2048, LN), BF16)],
        compiler_params=params(20),
        name="react",
        cost_estimate=COST,
    )(conc, cells, order, stoich, load, lr)


def diffuse(info_ref, which, a, b, ev, od, from_peer, from_chip, change, coef):
    me = info_ref[0]
    ring = info_ref[1]
    x_hi = (me >> 2) ^ which
    first = x_hi == 0
    own, other = (a, b) if which == 0 else (b, a)
    own, other = [v.astype(F32) for v in own], [v.astype(F32) for v in other]
    even = (ring & 1) == 0
    ev, od = ev.astype(F32), od.astype(F32)
    lo = jnp.where(ring == 0, own[0], jnp.where(even, od, ev))
    hi = jnp.where(ring == 15, own[1], jnp.where(even, ev, od))
    below = [jnp.where(first, lo, other[1]), own[0]]
    above = [own[1], jnp.where(first, other[0], hi)]
    rows = own[0].shape[0]
    lane = lax.broadcasted_iota(jnp.int32, (rows, 128), 1)
    low = lane < GY
    column = lane & (GY - 1)
    core = me & 1
    out = []
    for p in range(2):
        c = own[p]
        peer, chip = from_peer[p].astype(F32), from_chip[p].astype(F32)
        left, right = jnp.where(core == 0, chip, peer), jnp.where(core == 0, peer, chip)
        left = jnp.where(first, left, pltpu.roll(left, GY, 1))
        right = jnp.where(first, pltpu.roll(right, GY, 1), right)
        vs = [c[:, 128 * j:128 * j + 128] for j in range(LN // 128)]
        sw = [pltpu.roll(v, GY, 1) for v in vs]
        left = jnp.where(me == 0, vs[0], left)
        right = jnp.where(me == N - 1, vs[-1], right)
        lat = []
        for j, v in enumerate(vs):
            prev = left if j == 0 else sw[j - 1]
            nxt = right if j == len(vs) - 1 else sw[j + 1]
            x_dn = jnp.where(low, prev, sw[j])
            x_up = jnp.where(low, sw[j], nxt)
            y_up = jnp.where(column == GY - 1, v, pltpu.roll(v, 127, 1))
            y_dn = jnp.where(column == 0, v, pltpu.roll(v, 1, 1))
            lat.append(x_up + x_dn + y_up + y_dn)
        lap = above[p] + below[p] + jnp.concatenate(lat, axis=1) - 6.0 * c
        co = jnp.concatenate([coef] * (LN // 128), axis=1)
        out.append(jnp.maximum(c + co * lap + change[p], FLOOR))
    return out


def two(ref):
    return [ref[0], ref[1]]


def advance(info_ref, a_ref, b_ref, da_ref, db_ref, ev_ref, od_ref, peer_ref, chip_ref, coef_ref, na_ref, nb_ref, *edges):
    a, b = two(a_ref), two(b_ref)
    args = (ev_ref[...], od_ref[...], two(peer_ref), two(chip_ref))
    new = [diffuse(info_ref, w, a, b, *args, two(d), coef_ref[...]) for w, d in ((0, da_ref), (1, db_ref))]
    for v, ref in zip(new, (na_ref, nb_ref)):
        ref[0], ref[1] = v
    put_edges(info_ref, *new, *edges)


ROWS = 64


def specs_of(at):
    return dict(
        two=pl.BlockSpec((2, ROWS, LN), lambda s, i: (0, at(s, i), 0)),
        one=pl.BlockSpec((ROWS, LN), lambda s, i: (at(s, i), 0)),
        side=pl.BlockSpec((2, ROWS, 128), lambda s, i: (0, at(s, i), 0)),
        col=pl.BlockSpec((ROWS, 128), lambda s, i: (at(s, i), 0)),
    )


def advance_call(info, a, b, da, db, halos, coef):
    n = specs_of(lambda s, i: s)
    pair = jax.ShapeDtypeStruct((2, S, LN), F32)
    return pl.pallas_call(
        advance,
        grid_spec=pltpu.PrefetchScalarGridSpec(
            num_scalar_prefetch=1,
            grid=(S // ROWS,),
            in_specs=[n["two"]] * 4 + [n["one"]] * 2 + [n["side"]] * 2 + [n["col"]],
            out_specs=[n["two"]] * 2 + [n["one"]] * 2 + [n["side"]] * 2,
        ),
        out_shape=(pair, pair) + EDGES,
        compiler_params=params(12),
        name="advance",
        cost_estimate=COST,
    )(info, a, b, da, db, *halos, coef)


def finish(which, info_ref, a_ref, b_ref, d_ref, ev_ref, od_ref, peer_ref, chip_ref, coef_ref, *outs):
    new = diffuse(info_ref, which, two(a_ref), two(b_ref), ev_ref[...], od_ref[...], two(peer_ref), two(chip_ref),
                  two(d_ref), coef_ref[...])
    j = pl.program_id(0)
    each = 4 // len(outs)
    for n, ref in enumerate(outs):
        @pl.when(j // each == n)
        def _(ref=ref):
            ref[0, 0], ref[0, 1] = [v.astype(BF16) for v in new]


def finish_call(which, info, a, b, d, halos, coef, count):
    n = specs_of(lambda s, i: (i[0] & 3) ^ s)
    each = 4 // count
    m = jax.ShapeDtypeStruct((each, 2, SB, LN), BF16)
    return pl.pallas_call(
        functools.partial(finish, which),
        grid_spec=pltpu.PrefetchScalarGridSpec(
            num_scalar_prefetch=1,
            grid=(4,),
            in_specs=[n["two"]] * 3 + [n["one"]] * 2 + [n["side"]] * 2 + [n["col"]],
            out_specs=[
                pl.BlockSpec((1, 2, SB, LN), lambda s, i, n=n: (jnp.clip(s - each * n, 0, each - 1), 0, 0, 0))
                for n in range(count)
            ],
        ),
        out_shape=(m,) * count,
        compiler_params=params(12),
        name="finish",
        cost_estimate=COST,
    )(info, a, b, d, *halos, coef)


def join_out(at, info_ref, *refs):
    pieces, out_ref, buf, sem = refs[:N], refs[N], refs[N + 1], refs[N + 2]
    me = info_ref[0]
    copies = []
    for k in range(N):
        lanes = pl.ds(pl.multiple_of((me ^ k) * LN, LN), LN)
        for p in range(2):
            buf[k, p] = pieces[k][at[k], p].astype(F32)
            c = pltpu.make_async_copy(buf.at[k, p], out_ref.at[:, p, lanes], sem.at[k, p])
            c.start()
            copies.append(c)
    for c in copies:
        c.wait()


def join_call(info, pieces, at):
    return pl.pallas_call(
        functools.partial(join_out, at),
        out_shape=jax.ShapeDtypeStruct((SB, 2, N * LN), F32),
        in_specs=[SMEM] + [VMEM] * N,
        out_specs=pl.BlockSpec(memory_space=pl.ANY),
        scratch_shapes=[pltpu.VMEM((N, 2, SB, LN), F32), pltpu.SemaphoreType.DMA((N, 2))],
        compiler_params=params(12),
        name="join_out",
        cost_estimate=COST,
    )(info, *pieces)


def send(v, k):
    return lax.ppermute(v, RING, [(i, i ^ k) for i in range(N)])


def swap(v, axis, firsts):
    return lax.ppermute(v, axis, [(i, i + 1) for i in firsts] + [(i + 1, i) for i in firsts])


def exchange(edges):
    ev, od, peer, chip = edges
    return (
        swap(ev, "zy", range(0, 15, 2)),
        swap(od, "zy", range(1, 15, 2)),
        send(peer, 1),
        swap(chip, RING, (1, 3, 5)),
    )


def on_device(conc, order, stoich, species_class, diff_coef, rate, noise_load, cell_noise):
    info = jnp.stack([lax.axis_index(RING), lax.axis_index("zy")]).astype(jnp.int32)
    w = weights_call(
        order, stoich, jnp.transpose(noise_load, (0, 2, 1)), rate[None, :], species_class[None, :], diff_coef
    )
    far = lax.ppermute(w, RING, [(i, i ^ (6 if i % 2 else 2)) for i in range(N)])
    beside = send(w, 1)
    after_w, w = lax.optimization_barrier((info, w))
    mine, peer, inner, opp, outer, near = state_call(after_w, conc, cell_noise)
    far, mine = lax.optimization_barrier((far, mine))
    inner, opp, outer = send(inner, 2), send(opp, 4), send(outer, 6)
    ws = sort_call(info, [w, beside, far, *[send(far[:, lo:hi], 1) for lo, hi in zip(PARTS, PARTS[1:])]])
    inner, *ws = lax.optimization_barrier((inner, *ws))
    coef = ws[-1]
    a = gather_call(info, [mine, send(peer, 1), inner, send(inner[2 * SB:], 1)], (0, 0, 0, 0))
    da = react_call(0, a, near, ws)
    opp, outer, da = lax.optimization_barrier((opp, outer, da))
    cells = outer
    b = gather_call(info, [opp, send(opp, 1), outer, send(outer, 1)], (0, 2, 0, 2))
    around = exchange(edges_call(info, a, b))
    db = react_call(0, b, cells, ws, far=True)
    a, b, *edges = advance_call(info, a, b, da, db, around, coef)
    around = exchange(edges)
    db = react_call(1, b, cells, ws, far=True)
    opp, outer = finish_call(1, info, a, b, db, around, coef, 2)
    opp, outer, near = lax.optimization_barrier((opp, outer, near))
    opp, outer = send(opp, 4), send(outer, 6)
    da = react_call(1, a, near, ws)
    near_out = finish_call(0, info, a, b, da, around, coef, 4)
    back = [near_out[0]] + [send(near_out[k], k) for k in range(1, 4)]
    opp, outer, *back = lax.optimization_barrier((opp, outer, *back))
    back += [opp, send(opp, 1), outer, send(outer, 1)]
    return join_call(info, back, (0, 0, 0, 0, 0, 1, 0, 1))


def solution(mesh):
    grid = Mesh(mesh.devices.reshape(16, 2, 2, 2), ("zy", "x_hi", "x_lo", "core"))
    rxn, slab = ("x_lo", "core"), ("zy", "x_hi")
    placed = (
        P(rxn, slab, None),
        P(rxn, None),
        P(None, rxn),
        P(rxn),
        P(),
        P(rxn),
        P(None, rxn, None),
        P(None, None, slab, None),
    )
    return jax.shard_map(
        on_device, mesh=grid, in_specs=placed, out_specs=P(rxn, slab, None), check_vma=False
    )
```

```python
import functools

import jax
import jax.numpy as jnp
from jax import lax
from jax.experimental import pallas as pl
from jax.experimental.pallas import tpu as pltpu
from jax.sharding import Mesh, PartitionSpec as P

GY = 64
K = 32
STEPS = 2
S = 256
TAU = 0.1
FLOOR = 0.02
HALF_LOG2E = 0.7213475204444817

RING = ("x_hi", "x_lo", "core")
N = 8
SB = 64
LN = 512
FAR = 384
WROWS = 656

F32 = jnp.float32
BF16 = jnp.bfloat16
COST = pl.CostEstimate(flops=1, bytes_accessed=1, transcendentals=0)
VMEM = pl.BlockSpec(memory_space=pltpu.VMEM)
SMEM = pl.BlockSpec(memory_space=pltpu.SMEM)


def split2(v):
    hi = v.astype(BF16)
    return hi, (v - hi.astype(F32)).astype(BF16)


def split3(v):
    hi = v.astype(BF16)
    rest = v - hi.astype(F32)
    mid = rest.astype(BF16)
    return hi, mid, (rest - mid.astype(F32)).astype(BF16)


def pack_weights(order_ref, stoich_ref, load_ref, rate_ref, class_ref, coef_ref, w_ref):
    cls = class_ref[...]
    coef = jnp.zeros(cls.shape, F32)
    for c in range(coef_ref.shape[0]):
        coef = jnp.where(cls == c, coef_ref[c], coef)
    lr = 0.5 * jnp.log2(rate_ref[...] * TAU)
    lr3 = [v.astype(F32) for v in split3(lr)]
    co3 = [jnp.concatenate([v.astype(F32), jnp.zeros((1, 192), F32)], axis=1) for v in split3(coef * TAU)]
    for h in range(2):
        out = w_ref.at[h]
        rs = slice(h * 256, h * 256 + 256)
        out[0:256, :] = order_ref[rs, :].astype(F32).astype(BF16)
        out[256:512, :] = stoich_ref[:, rs].astype(F32).astype(BF16)
        for t in range(STEPS):
            hi, lo = split2(load_ref[t, :, rs] * (K ** -0.5))
            out[512 + 64 * t:544 + 64 * t, :] = hi
            out[544 + 64 * t:576 + 64 * t, :] = lo
        tail = jnp.concatenate([v[:, rs] for v in lr3] + co3 + [jnp.zeros((10, 256), F32)], axis=0)
        out[640:656, :] = tail.astype(BF16)


def params(mib):
    return pltpu.CompilerParams(vmem_limit_bytes=mib << 20)


def weights_call(order, stoich, load_t, rate, cls, coef):
    return pl.pallas_call(
        pack_weights,
        out_shape=jax.ShapeDtypeStruct((2, WROWS, 256), BF16),
        in_specs=[VMEM] * 5 + [SMEM],
        out_specs=VMEM,
        compiler_params=params(60),
        name="pack_weights",
        cost_estimate=COST,
    )(order, stoich, load_t, rate, cls, coef)


def pack_state(info_ref, conc_ref, cell_ref, self_ref, peer_ref, inner_ref, opp_ref, outer_ref, near_ref,
               buf, cells, sem, cell_sem):
    me = info_ref[0]
    order = (2, 3, 6, 7, 4, 5, 0, 1)
    places = {2: (inner_ref, 0), 3: (inner_ref, 2), 6: (outer_ref, 0), 7: (outer_ref, 2), 4: (opp_ref, 0),
              5: (opp_ref, 2), 0: (self_ref, 0), 1: (peer_ref, 0)}

    def lanes(k):
        return pl.ds(pl.multiple_of((me ^ k) * LN, LN), LN)

    copies = {}
    for k in order:
        for p in range(2):
            copies[k, p] = pltpu.make_async_copy(conc_ref.at[:, p, lanes(k)], buf.at[k, p], sem.at[k, p])
            copies[k, p].start()
    noise = {}
    for i, k in enumerate((6, 0)):
        for t in range(STEPS):
            for p in range(2):
                c = pltpu.make_async_copy(cell_ref.at[t, :, p, lanes(k)], cells.at[i, t, p], cell_sem.at[i, t, p])
                c.start()
                noise[i, t, p] = c
    for k in order:
        out, at = places[k]
        for p in range(2):
            copies[k, p].wait()
            out[SB * (at + p):SB * (at + p + 1)] = buf[k, p].astype(BF16)
    for t in range(STEPS):
        for p in range(2):
            for i in range(2):
                noise[i, t, p].wait()
            hi, lo = split2(cells[1, t, p])
            near_ref[t, p, 0:32] = hi
            near_ref[t, p, 32:64] = lo
            at = 4 * SB + 2 * K * t + K * p
            outer_ref[at:at + K] = cells[0, t, p].astype(BF16)


def state_call(info, conc, cell):
    def m(rows):
        return jax.ShapeDtypeStruct((rows, LN), BF16)

    any_ = pl.BlockSpec(memory_space=pl.ANY)
    return pl.pallas_call(
        pack_state,
        out_shape=(m(128), m(128), m(256), m(256), m(FAR), jax.ShapeDtypeStruct((STEPS, 2, SB, LN), BF16)),
        in_specs=[SMEM, any_, any_],
        out_specs=(VMEM,) * 6,
        scratch_shapes=[
            pltpu.VMEM((N, 2, SB, LN), F32),
            pltpu.VMEM((2, STEPS, 2, K, LN), F32),
            pltpu.SemaphoreType.DMA((N, 2)),
            pltpu.SemaphoreType.DMA((2, STEPS, 2)),
        ],
        compiler_params=params(60),
        name="pack_state",
        cost_estimate=COST,
    )(info, conc, cell)


PARTS = (0, 224, 448, WROWS)


def sort_weights(info_ref, *refs):
    own, beside, far, *parts = refs[:6]
    order_ref, stoich_ref, load_ref, lr_ref, coef_ref = refs[6:]
    me = info_ref[0]
    for i in range(N):
        def rows_of(start, stop, i=i):
            if i < 6:
                return (own, beside, far)[i // 2][i % 2, start:stop]
            cuts = [(max(start, lo) - lo, min(stop, hi) - lo) for lo, hi in zip(PARTS, PARTS[1:])]
            return jnp.concatenate([p[i % 2, lo:hi] for p, (lo, hi) in zip(parts, cuts) if lo < hi], axis=0)

        rows = pl.ds(i * 256, 256)
        order_ref[rows, :] = rows_of(0, 256)
        stoich_ref[:, rows] = rows_of(256, 512)
        loads = rows_of(512, WROWS).astype(F32)
        tail = loads[128:]
        for t in range(STEPS):
            hi, lo = loads[64 * t:64 * t + 32], loads[64 * t + 32:64 * t + 64]
            block = jnp.concatenate([hi, hi, lo, tail, jnp.zeros((16, 256), F32)], axis=0)
            turned = block.T
            lane = lax.broadcasted_iota(jnp.int32, turned.shape, 1)
            load_ref[t, rows, :] = jnp.where(lane < 96, turned, 0.0).astype(BF16)
        lr = turned[:, 96:97] + turned[:, 97:98] + turned[:, 98:99]
        lr_ref[rows, :] = jnp.broadcast_to(lr, (256, 128))
        if i % 2 == 0:
            co = turned[:SB, 99:100] + turned[:SB, 100:101] + turned[:SB, 101:102]
            at = pl.ds(pl.multiple_of(((me & 3) ^ (i // 2)) * SB, SB), SB)
            coef_ref[at, :] = jnp.broadcast_to(co, (SB, 128))


def sort_call(info, ws):
    return pl.pallas_call(
        sort_weights,
        out_shape=(
            jax.ShapeDtypeStruct((2048, S), BF16),
            jax.ShapeDtypeStruct((S, 2048), BF16),
            jax.ShapeDtypeStruct((STEPS, 2048, 128), BF16),
            jax.ShapeDtypeStruct((2048, 128), F32),
            jax.ShapeDtypeStruct((S, 128), F32),
        ),
        in_specs=[SMEM] + [VMEM] * 6,
        out_specs=(VMEM,) * 5,
        compiler_params=params(10),
        name="sort_weights",
        cost_estimate=COST,
    )(info, *ws)


def gather_planes(at, info_ref, *refs):
    pieces, out_ref = refs[:4], refs[4]
    me = info_ref[0]
    for j in range(4):
        rows = pl.ds(pl.multiple_of(((me & 3) ^ j) * SB, SB), SB)
        for p in range(2):
            out_ref[p, rows, :] = pieces[j][SB * (at[j] + p):SB * (at[j] + p + 1)]


def gather_call(info, pieces, at):
    return pl.pallas_call(
        functools.partial(gather_planes, at),
        out_shape=jax.ShapeDtypeStruct((2, S, LN), BF16),
        in_specs=[SMEM] + [VMEM] * 4,
        out_specs=VMEM,
        compiler_params=params(6),
        name="gather_planes",
        cost_estimate=COST,
    )(info, *pieces)


def put_edges(info_ref, a, b, ev_ref, od_ref, peer_ref, chip_ref, rows):
    me = info_ref[0]
    first = (me >> 2) == 0
    core = me & 1
    even = (info_ref[1] & 1) == 0
    lo = jnp.where(first, a[0].astype(F32), b[0].astype(F32))
    hi = jnp.where(first, b[1].astype(F32), a[1].astype(F32))
    ev_ref[rows, :] = jnp.where(even, hi, lo).astype(BF16)
    od_ref[rows, :] = jnp.where(even, lo, hi).astype(BF16)
    for q in range(2):
        sides = []
        for cut in (slice(0, 128), slice(LN - 128, LN)):
            va, vb = a[q][:, cut].astype(F32), b[q][:, cut].astype(F32)
            sides.append((jnp.where(first, va, vb), jnp.where(first, vb, va)))
        low = lax.broadcasted_iota(jnp.int32, sides[0][0].shape, 1) < GY
        left = jnp.where(low, sides[0][0], pltpu.roll(sides[0][1], GY, 1))
        right = jnp.where(low, pltpu.roll(sides[1][0], GY, 1), sides[1][1])
        peer_ref[q, rows, :] = jnp.where(core == 0, right, left).astype(BF16)
        chip_ref[q, rows, :] = jnp.where(core == 0, left, right).astype(BF16)


EDGES = (
    jax.ShapeDtypeStruct((S, LN), BF16),
    jax.ShapeDtypeStruct((S, LN), BF16),
    jax.ShapeDtypeStruct((2, S, 128), BF16),
    jax.ShapeDtypeStruct((2, S, 128), BF16),
)


def gather_far(at, info_ref, a_ref, *refs):
    pieces, out_ref, edges = refs[:4], refs[4], refs[5:]
    gather_planes(at, info_ref, *pieces, out_ref)

    def block(s, _):
        rows = pl.ds(pl.multiple_of(s * SB, SB), SB)
        put_edges(info_ref, [a_ref[0, rows, :], a_ref[1, rows, :]], [out_ref[0, rows, :], out_ref[1, rows, :]], *edges, rows)
        return 0

    lax.fori_loop(0, S // SB, block, 0)


def gather_far_call(info, a, pieces, at):
    return pl.pallas_call(
        functools.partial(gather_far, at),
        out_shape=(jax.ShapeDtypeStruct((2, S, LN), BF16),) + EDGES,
        in_specs=[SMEM] + [VMEM] * 5,
        out_specs=(VMEM,) * 5,
        compiler_params=params(6),
        name="gather_far",
        cost_estimate=COST,
    )(info, a, *pieces)


def react(far, conc_ref, cell_ref, order_ref, stoich_ref, load_ref, lr_ref, change_ref, flux_s):
    logs = jnp.log(conc_ref[0].astype(F32)).astype(BF16)
    zeros = jnp.zeros((K, LN), BF16)
    if far:
        hi, lo = cell_ref[...], zeros
    else:
        hi, lo = cell_ref[0, 0, :K], cell_ref[0, 0, K:]
    cells = jnp.concatenate([hi, lo, hi, zeros], axis=0)
    for i in range(N):
        rows = pl.ds(i * 256, 256)
        expo = jnp.dot(order_ref[rows, :], logs, preferred_element_type=F32)
        noise = jnp.dot(load_ref[0, rows, :], cells, preferred_element_type=F32)
        lr = lr_ref[rows, :]
        root = jnp.exp2(expo * HALF_LOG2E + jnp.concatenate([lr] * (LN // 128), axis=1))
        flux_s[rows, :] = (root * (root + noise)).astype(BF16)
    change_ref[0] = jnp.dot(stoich_ref[...], flux_s[...], preferred_element_type=F32)


def react_call(step, conc, cells, sorted_ws, far=False):
    order, stoich, load, lr, _ = sorted_ws
    plane = pl.BlockSpec((1, S, LN), lambda p: (p, 0, 0))
    if far:
        cell = pl.BlockSpec((K, LN), lambda p: (4 * SB // K + 2 * step + p, 0))
    else:
        cell = pl.BlockSpec((1, 1, 2 * K, LN), lambda p: (step, p, 0, 0))
    return pl.pallas_call(
        functools.partial(react, far),
        grid=(2,),
        out_shape=jax.ShapeDtypeStruct((2, S, LN), F32),
        in_specs=[
            plane,
            cell,
            pl.BlockSpec((2048, S), lambda p: (0, 0)),
            pl.BlockSpec((S, 2048), lambda p: (0, 0)),
            pl.BlockSpec((1, 2048, 128), lambda p: (step, 0, 0)),
            pl.BlockSpec((2048, 128), lambda p: (0, 0)),
        ],
        out_specs=plane,
        scratch_shapes=[pltpu.VMEM((2048, LN), BF16)],
        compiler_params=params(20),
        name="react",
        cost_estimate=COST,
    )(conc, cells, order, stoich, load, lr)


def diffuse(info_ref, which, a, b, ev, od, from_peer, from_chip, change, coef):
    me = info_ref[0]
    ring = info_ref[1]
    x_hi = (me >> 2) ^ which
    first = x_hi == 0
    own, other = (a, b) if which == 0 else (b, a)
    own, other = [v.astype(F32) for v in own], [v.astype(F32) for v in other]
    even = (ring & 1) == 0
    ev, od = ev.astype(F32), od.astype(F32)
    lo = jnp.where(ring == 0, own[0], jnp.where(even, od, ev))
    hi = jnp.where(ring == 15, own[1], jnp.where(even, ev, od))
    below = [jnp.where(first, lo, other[1]), own[0]]
    above = [own[1], jnp.where(first, other[0], hi)]
    rows = own[0].shape[0]
    lane = lax.broadcasted_iota(jnp.int32, (rows, 128), 1)
    low = lane < GY
    column = lane & (GY - 1)
    core = me & 1
    out = []
    for p in range(2):
        c = own[p]
        peer, chip = from_peer[p].astype(F32), from_chip[p].astype(F32)
        left, right = jnp.where(core == 0, chip, peer), jnp.where(core == 0, peer, chip)
        left = jnp.where(first, left, pltpu.roll(left, GY, 1))
        right = jnp.where(first, pltpu.roll(right, GY, 1), right)
        vs = [c[:, 128 * j:128 * j + 128] for j in range(LN // 128)]
        sw = [pltpu.roll(v, GY, 1) for v in vs]
        left = jnp.where(me == 0, vs[0], left)
        right = jnp.where(me == N - 1, vs[-1], right)
        lat = []
        for j, v in enumerate(vs):
            prev = left if j == 0 else sw[j - 1]
            nxt = right if j == len(vs) - 1 else sw[j + 1]
            x_dn = jnp.where(low, prev, sw[j])
            x_up = jnp.where(low, sw[j], nxt)
            y_up = jnp.where(column == GY - 1, v, pltpu.roll(v, 127, 1))
            y_dn = jnp.where(column == 0, v, pltpu.roll(v, 1, 1))
            lat.append(x_up + x_dn + y_up + y_dn)
        lap = above[p] + below[p] + jnp.concatenate(lat, axis=1) - 6.0 * c
        co = jnp.concatenate([coef] * (LN // 128), axis=1)
        out.append(jnp.maximum(c + co * lap + change[p], FLOOR))
    return out


def two(ref):
    return [ref[0], ref[1]]


ROWS = 32


def near_rows(rows, a_ref, b_ref, ev_ref, od_ref, peer_ref, chip_ref):
    def pair(ref):
        return [ref[0, rows, :], ref[1, rows, :]]

    return pair(a_ref), pair(b_ref), ev_ref[rows, :], od_ref[rows, :], pair(peer_ref), pair(chip_ref)


def advance(info_ref, a_ref, b_ref, da_ref, db_ref, ev_ref, od_ref, peer_ref, chip_ref, coef_ref, na_ref, nb_ref, *edges):
    def block(s, _):
        rows = pl.ds(pl.multiple_of(s * ROWS, ROWS), ROWS)
        args = near_rows(rows, a_ref, b_ref, ev_ref, od_ref, peer_ref, chip_ref)
        new = []
        for which, d_ref, out_ref in ((0, da_ref, na_ref), (1, db_ref, nb_ref)):
            new.append(diffuse(info_ref, which, *args, [d_ref[0, rows, :], d_ref[1, rows, :]], coef_ref[rows, :]))
            out_ref[0, rows, :], out_ref[1, rows, :] = new[-1]
        put_edges(info_ref, *new, *edges, rows)
        return 0

    lax.fori_loop(0, S // ROWS, block, 0, unroll=4)


def advance_call(info, a, b, da, db, halos, coef):
    pair = jax.ShapeDtypeStruct((2, S, LN), F32)
    return pl.pallas_call(
        advance,
        in_specs=[SMEM] + [VMEM] * 9,
        out_specs=(VMEM,) * 6,
        out_shape=(pair, pair) + EDGES,
        compiler_params=params(16),
        name="advance",
        cost_estimate=COST,
    )(info, a, b, da, db, *halos, coef)


def finish(which, info_ref, a_ref, b_ref, d_ref, ev_ref, od_ref, peer_ref, chip_ref, coef_ref, *outs):
    me = info_ref[0]
    places = [(ref, i) for ref in outs for i in range(ref.shape[0])]
    for j, (out, at) in enumerate(places):
        def block(s, _, j=j, out=out, at=at):
            rows = pl.ds(pl.multiple_of(((me & 3) ^ j) * SB + s * ROWS, ROWS), ROWS)
            to = pl.ds(pl.multiple_of(s * ROWS, ROWS), ROWS)
            args = near_rows(rows, a_ref, b_ref, ev_ref, od_ref, peer_ref, chip_ref)
            new = diffuse(info_ref, which, *args, [d_ref[0, rows, :], d_ref[1, rows, :]], coef_ref[rows, :])
            for p in range(2):
                out[at, p, to, :] = new[p].astype(BF16)
            return 0

        lax.fori_loop(0, SB // ROWS, block, 0, unroll=True)


def finish_call(which, info, a, b, d, halos, coef, counts):
    return pl.pallas_call(
        functools.partial(finish, which),
        in_specs=[SMEM] + [VMEM] * 8,
        out_specs=(VMEM,) * len(counts),
        out_shape=[jax.ShapeDtypeStruct((n, 2, SB, LN), BF16) for n in counts],
        compiler_params=params(12),
        name="finish",
        cost_estimate=COST,
    )(info, a, b, d, *halos, coef)


def join_out(at, info_ref, *refs):
    pieces, out_ref, buf, sem = refs[:N], refs[N], refs[N + 1], refs[N + 2]
    me = info_ref[0]
    copies = []
    for k in range(N):
        lanes = pl.ds(pl.multiple_of((me ^ k) * LN, LN), LN)
        for p in range(2):
            buf[k, p] = pieces[k][at[k], p].astype(F32)
            c = pltpu.make_async_copy(buf.at[k, p], out_ref.at[:, p, lanes], sem.at[k, p])
            c.start()
            copies.append(c)
    for c in copies:
        c.wait()


def join_call(info, pieces, at):
    return pl.pallas_call(
        functools.partial(join_out, at),
        out_shape=jax.ShapeDtypeStruct((SB, 2, N * LN), F32),
        in_specs=[SMEM] + [VMEM] * N,
        out_specs=pl.BlockSpec(memory_space=pl.ANY),
        scratch_shapes=[pltpu.VMEM((N, 2, SB, LN), F32), pltpu.SemaphoreType.DMA((N, 2))],
        compiler_params=params(12),
        name="join_out",
        cost_estimate=COST,
    )(info, *pieces)


def send(v, k):
    return lax.ppermute(v, RING, [(i, i ^ k) for i in range(N)])


def swap(v, axis, firsts):
    return lax.ppermute(v, axis, [(i, i + 1) for i in firsts] + [(i + 1, i) for i in firsts])


def exchange(edges):
    ev, od, peer, chip = edges
    od = swap(od, "zy", range(1, 15, 2))
    ev = swap(ev, "zy", range(0, 15, 2))
    return ev, od, send(peer, 1), swap(chip, RING, (1, 3, 5))


def on_device(conc, order, stoich, species_class, diff_coef, rate, noise_load, cell_noise):
    info = jnp.stack([lax.axis_index(RING), lax.axis_index("zy")]).astype(jnp.int32)
    w = weights_call(
        order, stoich, jnp.transpose(noise_load, (0, 2, 1)), rate[None, :], species_class[None, :], diff_coef
    )
    far = lax.ppermute(w, RING, [(i, i ^ (6 if i % 2 else 2)) for i in range(N)])
    beside = send(w, 1)
    after_w, w = lax.optimization_barrier((info, w))
    mine, peer, inner, opp, outer, near = state_call(after_w, conc, cell_noise)
    far, mine = lax.optimization_barrier((far, mine))
    inner, opp, outer = send(inner, 2), send(opp, 4), send(outer, 6)
    ws = sort_call(info, [w, beside, far, *[send(far[:, lo:hi], 1) for lo, hi in zip(PARTS, PARTS[1:])]])
    inner, *ws = lax.optimization_barrier((inner, *ws))
    coef = ws[-1]
    a = gather_call(info, [mine, send(peer, 1), inner, send(inner[2 * SB:], 1)], (0, 0, 0, 0))
    da = react_call(0, a, near, ws)
    opp, outer, da = lax.optimization_barrier((opp, outer, da))
    cells = outer
    b, *edges = gather_far_call(info, a, [opp, send(opp, 1), outer, send(outer, 1)], (0, 2, 0, 2))
    around = exchange(edges)
    db = react_call(0, b, cells, ws, far=True)
    a, b, *edges = advance_call(info, a, b, da, db, around, coef)
    around = exchange(edges)
    db = react_call(1, b, cells, ws, far=True)
    opp, outer = finish_call(1, info, a, b, db, around, coef, (2, 2))
    opp, outer, near = lax.optimization_barrier((opp, outer, near))
    opp, outer = send(opp, 4), send(outer, 6)
    da = react_call(1, a, near, ws)
    mine, peer, inner = finish_call(0, info, a, b, da, around, coef, (1, 1, 2))
    opp, outer, mine = lax.optimization_barrier((opp, outer, mine))
    inner = send(inner, 2)
    back = [mine, send(peer, 1), inner, send(inner[1:], 1), opp, send(opp, 1), outer, send(outer, 1)]
    return join_call(info, back, (0, 0, 0, 0, 0, 1, 0, 1))


def solution(mesh):
    grid = Mesh(mesh.devices.reshape(16, 2, 2, 2), ("zy", "x_hi", "x_lo", "core"))
    rxn, slab = ("x_lo", "core"), ("zy", "x_hi")
    placed = (
        P(rxn, slab, None),
        P(rxn, None),
        P(None, rxn),
        P(rxn),
        P(),
        P(rxn),
        P(None, rxn, None),
        P(None, None, slab, None),
    )
    return jax.shard_map(
        on_device, mesh=grid, in_specs=placed, out_specs=P(rxn, slab, None), check_vma=False
    )
```

```python
import functools

import jax
import jax.numpy as jnp
from jax import lax
from jax.experimental import pallas as pl
from jax.experimental.pallas import tpu as pltpu
from jax.sharding import Mesh, PartitionSpec as P

GY = 64
K = 32
STEPS = 2
S = 256
TAU = 0.1
FLOOR = 0.02
HALF_LOG2E = 0.7213475204444817

RING = ("x_hi", "x_lo", "core")
N = 8
SB = 64
LN = 512
FAR = 384
WROWS = 656

F32 = jnp.float32
BF16 = jnp.bfloat16
COST = pl.CostEstimate(flops=1, bytes_accessed=1, transcendentals=0)
VMEM = pl.BlockSpec(memory_space=pltpu.VMEM)
SMEM = pl.BlockSpec(memory_space=pltpu.SMEM)


def split2(v):
    hi = v.astype(BF16)
    return hi, (v - hi.astype(F32)).astype(BF16)


def split3(v):
    hi = v.astype(BF16)
    rest = v - hi.astype(F32)
    mid = rest.astype(BF16)
    return hi, mid, (rest - mid.astype(F32)).astype(BF16)


def pack_weights(order_ref, stoich_ref, load_ref, rate_ref, class_ref, coef_ref, w_ref):
    cls = class_ref[...]
    coef = jnp.zeros(cls.shape, F32)
    for c in range(coef_ref.shape[0]):
        coef = jnp.where(cls == c, coef_ref[c], coef)
    lr = 0.5 * jnp.log2(rate_ref[...] * TAU)
    lr3 = [v.astype(F32) for v in split3(lr)]
    co3 = [jnp.concatenate([v.astype(F32), jnp.zeros((1, 192), F32)], axis=1) for v in split3(coef * TAU)]
    for h in range(2):
        out = w_ref.at[h]
        rs = slice(h * 256, h * 256 + 256)
        out[0:256, :] = order_ref[rs, :].astype(F32).astype(BF16)
        out[256:512, :] = stoich_ref[:, rs].astype(F32).astype(BF16)
        for t in range(STEPS):
            hi, lo = split2(load_ref[t, :, rs] * (K ** -0.5))
            out[512 + 64 * t:544 + 64 * t, :] = hi
            out[544 + 64 * t:576 + 64 * t, :] = lo
        tail = jnp.concatenate([v[:, rs] for v in lr3] + co3 + [jnp.zeros((10, 256), F32)], axis=0)
        out[640:656, :] = tail.astype(BF16)


def params(mib):
    return pltpu.CompilerParams(vmem_limit_bytes=mib << 20)


def weights_call(order, stoich, load_t, rate, cls, coef):
    return pl.pallas_call(
        pack_weights,
        out_shape=jax.ShapeDtypeStruct((2, WROWS, 256), BF16),
        in_specs=[VMEM] * 5 + [SMEM],
        out_specs=VMEM,
        compiler_params=params(60),
        name="pack_weights",
        cost_estimate=COST,
    )(order, stoich, load_t, rate, cls, coef)


def pack_state(info_ref, conc_ref, cell_ref, self_ref, peer_ref, inner_ref, opp_ref, outer_ref, near_ref,
               buf, cells, sem, cell_sem):
    me = info_ref[0]
    order = (2, 3, 6, 7, 4, 5, 0, 1)
    places = {2: (inner_ref, 0), 3: (inner_ref, 2), 6: (outer_ref, 0), 7: (outer_ref, 2), 4: (opp_ref, 0),
              5: (opp_ref, 2), 0: (self_ref, 0), 1: (peer_ref, 0)}

    def lanes(k):
        return pl.ds(pl.multiple_of((me ^ k) * LN, LN), LN)

    copies = {}
    for k in order:
        for p in range(2):
            copies[k, p] = pltpu.make_async_copy(conc_ref.at[:, p, lanes(k)], buf.at[k, p], sem.at[k, p])
            copies[k, p].start()
    noise = {}
    for i, k in enumerate((6, 0)):
        for t in range(STEPS):
            for p in range(2):
                c = pltpu.make_async_copy(cell_ref.at[t, :, p, lanes(k)], cells.at[i, t, p], cell_sem.at[i, t, p])
                c.start()
                noise[i, t, p] = c
    for k in order:
        out, at = places[k]
        for p in range(2):
            copies[k, p].wait()
            out[SB * (at + p):SB * (at + p + 1)] = buf[k, p].astype(BF16)
    for t in range(STEPS):
        for p in range(2):
            for i in range(2):
                noise[i, t, p].wait()
            hi, lo = split2(cells[1, t, p])
            near_ref[t, p, 0:32] = hi
            near_ref[t, p, 32:64] = lo
            at = 4 * SB + 2 * K * t + K * p
            outer_ref[at:at + K] = cells[0, t, p].astype(BF16)


def state_call(info, conc, cell):
    def m(rows):
        return jax.ShapeDtypeStruct((rows, LN), BF16)

    any_ = pl.BlockSpec(memory_space=pl.ANY)
    return pl.pallas_call(
        pack_state,
        out_shape=(m(128), m(128), m(256), m(256), m(FAR), jax.ShapeDtypeStruct((STEPS, 2, SB, LN), BF16)),
        in_specs=[SMEM, any_, any_],
        out_specs=(VMEM,) * 6,
        scratch_shapes=[
            pltpu.VMEM((N, 2, SB, LN), F32),
            pltpu.VMEM((2, STEPS, 2, K, LN), F32),
            pltpu.SemaphoreType.DMA((N, 2)),
            pltpu.SemaphoreType.DMA((2, STEPS, 2)),
        ],
        compiler_params=params(60),
        name="pack_state",
        cost_estimate=COST,
    )(info, conc, cell)


PARTS = (0, 224, 448, WROWS)


def sort_weights(info_ref, *refs):
    own, beside, far, *parts = refs[:6]
    order_ref, stoich_ref, load_ref, lr_ref, coef_ref = refs[6:]
    me = info_ref[0]
    for i in range(N):
        def rows_of(start, stop, i=i):
            if i < 6:
                return (own, beside, far)[i // 2][i % 2, start:stop]
            cuts = [(max(start, lo) - lo, min(stop, hi) - lo) for lo, hi in zip(PARTS, PARTS[1:])]
            return jnp.concatenate([p[i % 2, lo:hi] for p, (lo, hi) in zip(parts, cuts) if lo < hi], axis=0)

        rows = pl.ds(i * 256, 256)
        order_ref[rows, :] = rows_of(0, 256)
        stoich_ref[:, rows] = rows_of(256, 512)
        loads = rows_of(512, WROWS).astype(F32)
        tail = loads[128:]
        for t in range(STEPS):
            hi, lo = loads[64 * t:64 * t + 32], loads[64 * t + 32:64 * t + 64]
            block = jnp.concatenate([hi, hi, lo, tail, jnp.zeros((16, 256), F32)], axis=0)
            turned = block.T
            lane = lax.broadcasted_iota(jnp.int32, turned.shape, 1)
            load_ref[t, rows, :] = jnp.where(lane < 96, turned, 0.0).astype(BF16)
        lr = turned[:, 96:97] + turned[:, 97:98] + turned[:, 98:99]
        lr_ref[rows, :] = jnp.broadcast_to(lr, (256, 128))
        if i % 2 == 0:
            co = turned[:SB, 99:100] + turned[:SB, 100:101] + turned[:SB, 101:102]
            at = pl.ds(pl.multiple_of(((me & 3) ^ (i // 2)) * SB, SB), SB)
            coef_ref[at, :] = jnp.broadcast_to(co, (SB, 128))


def sort_call(info, ws):
    return pl.pallas_call(
        sort_weights,
        out_shape=(
            jax.ShapeDtypeStruct((2048, S), BF16),
            jax.ShapeDtypeStruct((S, 2048), BF16),
            jax.ShapeDtypeStruct((STEPS, 2048, 128), BF16),
            jax.ShapeDtypeStruct((2048, 128), F32),
            jax.ShapeDtypeStruct((S, 128), F32),
        ),
        in_specs=[SMEM] + [VMEM] * 6,
        out_specs=(VMEM,) * 5,
        compiler_params=params(10),
        name="sort_weights",
        cost_estimate=COST,
    )(info, *ws)


def gather_planes(at, info_ref, *refs):
    pieces, out_ref = refs[:4], refs[4]
    me = info_ref[0]
    for j in range(4):
        rows = pl.ds(pl.multiple_of(((me & 3) ^ j) * SB, SB), SB)
        for p in range(2):
            out_ref[p, rows, :] = pieces[j][SB * (at[j] + p):SB * (at[j] + p + 1)]


def gather_call(info, pieces, at):
    return pl.pallas_call(
        functools.partial(gather_planes, at),
        out_shape=jax.ShapeDtypeStruct((2, S, LN), BF16),
        in_specs=[SMEM] + [VMEM] * 4,
        out_specs=VMEM,
        compiler_params=params(6),
        name="gather_planes",
        cost_estimate=COST,
    )(info, *pieces)


def by_place(info_ref, body):
    for even in (True, False):
        for first in (True, False):
            here = ((info_ref[1] & 1) == (0 if even else 1)) & ((info_ref[0] >> 2) == (0 if first else 1))

            @pl.when(here)
            def _(even=even, first=first):
                body(even, first)


def put_edges(info_ref, place, a, b, ev_ref, od_ref, peer_ref, chip_ref, rows):
    even, first = place
    core = info_ref[0] & 1
    one, two = (a, b) if first else (b, a)
    ev, od = (two[1], one[0]) if even else (one[0], two[1])
    ev_ref[rows, :] = ev.astype(BF16)
    od_ref[rows, :] = od.astype(BF16)
    for q in range(2):
        sides = [(one[q][:, cut].astype(F32), two[q][:, cut].astype(F32)) for cut in (slice(0, 128), slice(LN - 128, LN))]
        low = lax.broadcasted_iota(jnp.int32, sides[0][0].shape, 1) < GY
        left = jnp.where(low, sides[0][0], pltpu.roll(sides[0][1], GY, 1))
        right = jnp.where(low, pltpu.roll(sides[1][0], GY, 1), sides[1][1])
        peer_ref[q, rows, :] = jnp.where(core == 0, right, left).astype(BF16)
        chip_ref[q, rows, :] = jnp.where(core == 0, left, right).astype(BF16)


EDGES = (
    jax.ShapeDtypeStruct((S, LN), BF16),
    jax.ShapeDtypeStruct((S, LN), BF16),
    jax.ShapeDtypeStruct((2, S, 128), BF16),
    jax.ShapeDtypeStruct((2, S, 128), BF16),
)


def gather_far(at, info_ref, a_ref, *refs):
    pieces, out_ref, edges = refs[:4], refs[4], refs[5:]
    gather_planes(at, info_ref, *pieces, out_ref)

    def body(*place):
        def block(s, _):
            rows = pl.ds(pl.multiple_of(s * SB, SB), SB)
            a, b = [[ref[0, rows, :], ref[1, rows, :]] for ref in (a_ref, out_ref)]
            put_edges(info_ref, place, a, b, *edges, rows)
            return 0

        lax.fori_loop(0, S // SB, block, 0, unroll=2)

    by_place(info_ref, body)


def gather_far_call(info, a, pieces, at):
    return pl.pallas_call(
        functools.partial(gather_far, at),
        out_shape=(jax.ShapeDtypeStruct((2, S, LN), BF16),) + EDGES,
        in_specs=[SMEM] + [VMEM] * 5,
        out_specs=(VMEM,) * 5,
        compiler_params=params(6),
        name="gather_far",
        cost_estimate=COST,
    )(info, a, *pieces)


def react(far, conc_ref, cell_ref, order_ref, stoich_ref, load_ref, lr_ref, change_ref, flux_s):
    logs = jnp.log(conc_ref[0].astype(F32)).astype(BF16)
    zeros = jnp.zeros((K, LN), BF16)
    if far:
        hi, lo = cell_ref[...], zeros
    else:
        hi, lo = cell_ref[0, 0, :K], cell_ref[0, 0, K:]
    cells = jnp.concatenate([hi, lo, hi, zeros], axis=0)
    for i in range(N):
        rows = pl.ds(i * 256, 256)
        expo = jnp.dot(order_ref[rows, :], logs, preferred_element_type=F32)
        noise = jnp.dot(load_ref[0, rows, :], cells, preferred_element_type=F32)
        lr = lr_ref[rows, :]
        root = jnp.exp2(expo * HALF_LOG2E + jnp.concatenate([lr] * (LN // 128), axis=1))
        flux_s[rows, :] = (root * (root + noise)).astype(BF16)
    change_ref[0] = jnp.dot(stoich_ref[...], flux_s[...], preferred_element_type=F32)


def react_call(step, conc, cells, sorted_ws, far=False):
    order, stoich, load, lr, _ = sorted_ws
    plane = pl.BlockSpec((1, S, LN), lambda p: (p, 0, 0))
    if far:
        cell = pl.BlockSpec((K, LN), lambda p: (4 * SB // K + 2 * step + p, 0))
    else:
        cell = pl.BlockSpec((1, 1, 2 * K, LN), lambda p: (step, p, 0, 0))
    return pl.pallas_call(
        functools.partial(react, far),
        grid=(2,),
        out_shape=jax.ShapeDtypeStruct((2, S, LN), F32),
        in_specs=[
            plane,
            cell,
            pl.BlockSpec((2048, S), lambda p: (0, 0)),
            pl.BlockSpec((S, 2048), lambda p: (0, 0)),
            pl.BlockSpec((1, 2048, 128), lambda p: (step, 0, 0)),
            pl.BlockSpec((2048, 128), lambda p: (0, 0)),
        ],
        out_specs=plane,
        scratch_shapes=[pltpu.VMEM((2048, LN), BF16)],
        compiler_params=params(20),
        name="react",
        cost_estimate=COST,
    )(conc, cells, order, stoich, load, lr)


def diffuse(info_ref, place, which, a, b, ev, od, from_peer, from_chip, change, coef):
    me = info_ref[0]
    ring = info_ref[1]
    even, first = place[0], place[1] == (which == 0)
    own, other = (a, b) if which == 0 else (b, a)
    own, other = [v.astype(F32) for v in own], [v.astype(F32) for v in other]
    if first:
        lo = jnp.where(ring == 0, own[0], (od if even else ev).astype(F32))
        below, above = [lo, own[0]], [own[1], other[0]]
    else:
        hi = jnp.where(ring == 15, own[1], (ev if even else od).astype(F32))
        below, above = [other[1], own[0]], [own[1], hi]
    rows = own[0].shape[0]
    lane = lax.broadcasted_iota(jnp.int32, (rows, 128), 1)
    low = lane < GY
    column = lane & (GY - 1)
    core = me & 1
    out = []
    for p in range(2):
        c = own[p]
        peer, chip = from_peer[p].astype(F32), from_chip[p].astype(F32)
        left, right = jnp.where(core == 0, chip, peer), jnp.where(core == 0, peer, chip)
        if first:
            right = pltpu.roll(right, GY, 1)
        else:
            left = pltpu.roll(left, GY, 1)
        vs = [c[:, 128 * j:128 * j + 128] for j in range(LN // 128)]
        vb = [v.astype(BF16) for v in vs]
        sw = [pltpu.roll(v, GY, 1).astype(F32) for v in vb]
        left = jnp.where(me == 0, vs[0], left)
        right = jnp.where(me == N - 1, vs[-1], right)
        lat = []
        for j, v in enumerate(vs):
            prev = left if j == 0 else sw[j - 1]
            nxt = right if j == len(vs) - 1 else sw[j + 1]
            x_dn = jnp.where(low, prev, sw[j])
            x_up = jnp.where(low, sw[j], nxt)
            y_up = jnp.where(column == GY - 1, v, pltpu.roll(vb[j], 127, 1).astype(F32))
            y_dn = jnp.where(column == 0, v, pltpu.roll(vb[j], 1, 1).astype(F32))
            lat.append(x_up + x_dn + y_up + y_dn)
        lap = above[p] + below[p] + jnp.concatenate(lat, axis=1) - 6.0 * c
        co = jnp.concatenate([coef] * (LN // 128), axis=1)
        out.append(jnp.maximum(c + co * lap + change[p], FLOOR))
    return out


def two(ref):
    return [ref[0], ref[1]]


ROWS = 32


def near_rows(rows, a_ref, b_ref, ev_ref, od_ref, peer_ref, chip_ref):
    def pair(ref):
        return [ref[0, rows, :], ref[1, rows, :]]

    return pair(a_ref), pair(b_ref), ev_ref[rows, :], od_ref[rows, :], pair(peer_ref), pair(chip_ref)


def advance(info_ref, a_ref, b_ref, da_ref, db_ref, ev_ref, od_ref, peer_ref, chip_ref, coef_ref, na_ref, nb_ref, *edges):
    def body(*place):
        def block(s, _):
            rows = pl.ds(pl.multiple_of(s * ROWS, ROWS), ROWS)
            args = near_rows(rows, a_ref, b_ref, ev_ref, od_ref, peer_ref, chip_ref)
            new = []
            for which, d_ref, out_ref in ((0, da_ref, na_ref), (1, db_ref, nb_ref)):
                change = [d_ref[0, rows, :], d_ref[1, rows, :]]
                new.append(diffuse(info_ref, place, which, *args, change, coef_ref[rows, :]))
                out_ref[0, rows, :], out_ref[1, rows, :] = new[-1]
            put_edges(info_ref, place, *new, *edges, rows)
            return 0

        lax.fori_loop(0, S // ROWS, block, 0, unroll=4)

    by_place(info_ref, body)


def advance_call(info, a, b, da, db, halos, coef):
    pair = jax.ShapeDtypeStruct((2, S, LN), F32)
    return pl.pallas_call(
        advance,
        in_specs=[SMEM] + [VMEM] * 9,
        out_specs=(VMEM,) * 6,
        out_shape=(pair, pair) + EDGES,
        compiler_params=params(16),
        name="advance",
        cost_estimate=COST,
    )(info, a, b, da, db, *halos, coef)


def finish(which, info_ref, a_ref, b_ref, d_ref, ev_ref, od_ref, peer_ref, chip_ref, coef_ref, *outs):
    me = info_ref[0]
    places = [(ref, i) for ref in outs for i in range(ref.shape[0])]

    def body(*place):
        for j, (out, at) in enumerate(places):
            for s in range(SB // ROWS):
                rows = pl.ds(pl.multiple_of(((me & 3) ^ j) * SB + s * ROWS, ROWS), ROWS)
                args = near_rows(rows, a_ref, b_ref, ev_ref, od_ref, peer_ref, chip_ref)
                new = diffuse(info_ref, place, which, *args, [d_ref[0, rows, :], d_ref[1, rows, :]], coef_ref[rows, :])
                for p in range(2):
                    out[at, p, s * ROWS:(s + 1) * ROWS, :] = new[p].astype(BF16)

    by_place(info_ref, body)


def finish_call(which, info, a, b, d, halos, coef, counts):
    return pl.pallas_call(
        functools.partial(finish, which),
        in_specs=[SMEM] + [VMEM] * 8,
        out_specs=(VMEM,) * len(counts),
        out_shape=[jax.ShapeDtypeStruct((n, 2, SB, LN), BF16) for n in counts],
        compiler_params=params(12),
        name="finish",
        cost_estimate=COST,
    )(info, a, b, d, *halos, coef)


def join_out(at, info_ref, *refs):
    pieces, out_ref, buf, sem = refs[:N], refs[N], refs[N + 1], refs[N + 2]
    me = info_ref[0]
    copies = []
    for k in range(N):
        lanes = pl.ds(pl.multiple_of((me ^ k) * LN, LN), LN)
        for p in range(2):
            buf[k, p] = pieces[k][at[k], p].astype(F32)
            c = pltpu.make_async_copy(buf.at[k, p], out_ref.at[:, p, lanes], sem.at[k, p])
            c.start()
            copies.append(c)
    for c in copies:
        c.wait()


def join_call(info, pieces, at):
    return pl.pallas_call(
        functools.partial(join_out, at),
        out_shape=jax.ShapeDtypeStruct((SB, 2, N * LN), F32),
        in_specs=[SMEM] + [VMEM] * N,
        out_specs=pl.BlockSpec(memory_space=pl.ANY),
        scratch_shapes=[pltpu.VMEM((N, 2, SB, LN), F32), pltpu.SemaphoreType.DMA((N, 2))],
        compiler_params=params(12),
        name="join_out",
        cost_estimate=COST,
    )(info, *pieces)


def send(v, k):
    return lax.ppermute(v, RING, [(i, i ^ k) for i in range(N)])


def swap(v, axis, firsts):
    return lax.ppermute(v, axis, [(i, i + 1) for i in firsts] + [(i + 1, i) for i in firsts])


def exchange(edges):
    ev, od, peer, chip = edges
    od = swap(od, "zy", range(1, 15, 2))
    ev = swap(ev, "zy", range(0, 15, 2))
    return ev, od, send(peer, 1), swap(chip, RING, (1, 3, 5))


def on_device(conc, order, stoich, species_class, diff_coef, rate, noise_load, cell_noise):
    info = jnp.stack([lax.axis_index(RING), lax.axis_index("zy")]).astype(jnp.int32)
    w = weights_call(
        order, stoich, jnp.transpose(noise_load, (0, 2, 1)), rate[None, :], species_class[None, :], diff_coef
    )
    far = lax.ppermute(w, RING, [(i, i ^ (6 if i % 2 else 2)) for i in range(N)])
    beside = send(w, 1)
    after_w, w = lax.optimization_barrier((info, w))
    mine, peer, inner, opp, outer, near = state_call(after_w, conc, cell_noise)
    far, mine = lax.optimization_barrier((far, mine))
    inner, opp, outer = send(inner, 2), send(opp, 4), send(outer, 6)
    ws = sort_call(info, [w, beside, far, *[send(far[:, lo:hi], 1) for lo, hi in zip(PARTS, PARTS[1:])]])
    inner, *ws = lax.optimization_barrier((inner, *ws))
    coef = ws[-1]
    a = gather_call(info, [mine, send(peer, 1), inner, send(inner[2 * SB:], 1)], (0, 0, 0, 0))
    da = react_call(0, a, near, ws)
    opp, outer, da = lax.optimization_barrier((opp, outer, da))
    cells = outer
    b, *edges = gather_far_call(info, a, [opp, send(opp, 1), outer, send(outer, 1)], (0, 2, 0, 2))
    around = exchange(edges)
    db = react_call(0, b, cells, ws, far=True)
    a, b, *edges = advance_call(info, a, b, da, db, around, coef)
    around = exchange(edges)
    db = react_call(1, b, cells, ws, far=True)
    opp, outer = finish_call(1, info, a, b, db, around, coef, (2, 2))
    opp, outer, near = lax.optimization_barrier((opp, outer, near))
    opp, outer = send(opp, 4), send(outer, 6)
    da = react_call(1, a, near, ws)
    mine, peer, inner = finish_call(0, info, a, b, da, around, coef, (1, 1, 2))
    opp, outer, mine = lax.optimization_barrier((opp, outer, mine))
    inner = send(inner, 2)
    back = [mine, send(peer, 1), inner, send(inner[1:], 1), opp, send(opp, 1), outer, send(outer, 1)]
    return join_call(info, back, (0, 0, 0, 0, 0, 1, 0, 1))


def solution(mesh):
    grid = Mesh(mesh.devices.reshape(16, 2, 2, 2), ("zy", "x_hi", "x_lo", "core"))
    rxn, slab = ("x_lo", "core"), ("zy", "x_hi")
    placed = (
        P(rxn, slab, None),
        P(rxn, None),
        P(None, rxn),
        P(rxn),
        P(),
        P(rxn),
        P(None, rxn, None),
        P(None, None, slab, None),
    )
    return jax.shard_map(
        on_device, mesh=grid, in_specs=placed, out_specs=P(rxn, slab, None), check_vma=False
    )
```

```python
import functools

import jax
import jax.numpy as jnp
from jax import lax
from jax.experimental import pallas as pl
from jax.experimental.pallas import tpu as pltpu
from jax.sharding import Mesh, PartitionSpec as P

GY = 64
K = 32
STEPS = 2
S = 256
TAU = 0.1
FLOOR = 0.02
HALF_LOG2E = 0.7213475204444817

RING = ("x_hi", "x_lo", "core")
N = 8
SB = 64
LN = 512
FAR = 384
WROWS = 656

F32 = jnp.float32
BF16 = jnp.bfloat16
COST = pl.CostEstimate(flops=1, bytes_accessed=1, transcendentals=0)
VMEM = pl.BlockSpec(memory_space=pltpu.VMEM)
SMEM = pl.BlockSpec(memory_space=pltpu.SMEM)


def split2(v):
    hi = v.astype(BF16)
    return hi, (v - hi.astype(F32)).astype(BF16)


def split3(v):
    hi = v.astype(BF16)
    rest = v - hi.astype(F32)
    mid = rest.astype(BF16)
    return hi, mid, (rest - mid.astype(F32)).astype(BF16)


def pack_weights(order_ref, stoich_ref, load_ref, rate_ref, class_ref, coef_ref, w_ref):
    cls = class_ref[...]
    coef = jnp.zeros(cls.shape, F32)
    for c in range(coef_ref.shape[0]):
        coef = jnp.where(cls == c, coef_ref[c], coef)
    lr = 0.5 * jnp.log2(rate_ref[...] * TAU)
    lr3 = [v.astype(F32) for v in split3(lr)]
    co3 = [jnp.concatenate([v.astype(F32), jnp.zeros((1, 192), F32)], axis=1) for v in split3(coef * TAU)]
    for h in range(2):
        out = w_ref.at[h]
        rs = slice(h * 256, h * 256 + 256)
        out[0:256, :] = order_ref[rs, :].astype(F32).astype(BF16)
        out[256:512, :] = stoich_ref[:, rs].astype(F32).astype(BF16)
        for t in range(STEPS):
            hi, lo = split2(load_ref[t, :, rs] * (K ** -0.5))
            out[512 + 64 * t:544 + 64 * t, :] = hi
            out[544 + 64 * t:576 + 64 * t, :] = lo
        tail = jnp.concatenate([v[:, rs] for v in lr3] + co3 + [jnp.zeros((10, 256), F32)], axis=0)
        out[640:656, :] = tail.astype(BF16)


def params(mib):
    return pltpu.CompilerParams(vmem_limit_bytes=mib << 20)


def weights_call(order, stoich, load_t, rate, cls, coef):
    return pl.pallas_call(
        pack_weights,
        out_shape=jax.ShapeDtypeStruct((2, WROWS, 256), BF16),
        in_specs=[VMEM] * 5 + [SMEM],
        out_specs=VMEM,
        compiler_params=params(60),
        name="pack_weights",
        cost_estimate=COST,
    )(order, stoich, load_t, rate, cls, coef)


def pack_state(info_ref, conc_ref, cell_ref, self_ref, peer_ref, inner_ref, opp_ref, outer_ref, near_ref,
               buf, cells, sem, cell_sem):
    me = info_ref[0]
    order = (2, 3, 6, 7, 4, 5, 0, 1)
    places = {2: (inner_ref, 0), 3: (inner_ref, 2), 6: (outer_ref, 0), 7: (outer_ref, 2), 4: (opp_ref, 0),
              5: (opp_ref, 2), 0: (self_ref, 0), 1: (peer_ref, 0)}

    def lanes(k):
        return pl.ds(pl.multiple_of((me ^ k) * LN, LN), LN)

    copies = {}
    for k in order:
        for p in range(2):
            copies[k, p] = pltpu.make_async_copy(conc_ref.at[:, p, lanes(k)], buf.at[k, p], sem.at[k, p])
            copies[k, p].start()
    noise = {}
    for i, k in enumerate((6, 0)):
        for t in range(STEPS):
            for p in range(2):
                c = pltpu.make_async_copy(cell_ref.at[t, :, p, lanes(k)], cells.at[i, t, p], cell_sem.at[i, t, p])
                c.start()
                noise[i, t, p] = c
    for k in order:
        out, at = places[k]
        for p in range(2):
            copies[k, p].wait()
            out[SB * (at + p):SB * (at + p + 1)] = buf[k, p].astype(BF16)
    for t in range(STEPS):
        for p in range(2):
            for i in range(2):
                noise[i, t, p].wait()
            hi, lo = split2(cells[1, t, p])
            near_ref[t, p, 0:32] = hi
            near_ref[t, p, 32:64] = lo
            at = 4 * SB + 2 * K * t + K * p
            outer_ref[at:at + K] = cells[0, t, p].astype(BF16)


def state_call(info, conc, cell):
    def m(rows):
        return jax.ShapeDtypeStruct((rows, LN), BF16)

    any_ = pl.BlockSpec(memory_space=pl.ANY)
    return pl.pallas_call(
        pack_state,
        out_shape=(m(128), m(128), m(256), m(256), m(FAR), jax.ShapeDtypeStruct((STEPS, 2, SB, LN), BF16)),
        in_specs=[SMEM, any_, any_],
        out_specs=(VMEM,) * 6,
        scratch_shapes=[
            pltpu.VMEM((N, 2, SB, LN), F32),
            pltpu.VMEM((2, STEPS, 2, K, LN), F32),
            pltpu.SemaphoreType.DMA((N, 2)),
            pltpu.SemaphoreType.DMA((2, STEPS, 2)),
        ],
        compiler_params=params(60),
        name="pack_state",
        cost_estimate=COST,
    )(info, conc, cell)


PARTS = (0, 224, 448, WROWS)


def sort_weights(info_ref, *refs):
    own, beside, far, *parts = refs[:6]
    order_ref, stoich_ref, load_ref, lr_ref, coef_ref = refs[6:]
    me = info_ref[0]
    for i in range(N):
        def rows_of(start, stop, i=i):
            if i < 6:
                return (own, beside, far)[i // 2][i % 2, start:stop]
            cuts = [(max(start, lo) - lo, min(stop, hi) - lo) for lo, hi in zip(PARTS, PARTS[1:])]
            return jnp.concatenate([p[i % 2, lo:hi] for p, (lo, hi) in zip(parts, cuts) if lo < hi], axis=0)

        rows = pl.ds(i * 256, 256)
        order_ref[rows, :] = rows_of(0, 256)
        stoich_ref[:, rows] = rows_of(256, 512)
        loads = rows_of(512, WROWS).astype(F32)
        tail = loads[128:]
        for t in range(STEPS):
            hi, lo = loads[64 * t:64 * t + 32], loads[64 * t + 32:64 * t + 64]
            block = jnp.concatenate([hi, hi, lo, tail, jnp.zeros((16, 256), F32)], axis=0)
            turned = block.T
            lane = lax.broadcasted_iota(jnp.int32, turned.shape, 1)
            load_ref[t, rows, :] = jnp.where(lane < 96, turned, 0.0).astype(BF16)
        lr = turned[:, 96:97] + turned[:, 97:98] + turned[:, 98:99]
        lr_ref[rows, :] = jnp.broadcast_to(lr, (256, 128))
        if i % 2 == 0:
            co = turned[:SB, 99:100] + turned[:SB, 100:101] + turned[:SB, 101:102]
            at = pl.ds(pl.multiple_of(((me & 3) ^ (i // 2)) * SB, SB), SB)
            coef_ref[at, :] = jnp.broadcast_to(co, (SB, 128))


def sort_call(info, ws):
    return pl.pallas_call(
        sort_weights,
        out_shape=(
            jax.ShapeDtypeStruct((2048, S), BF16),
            jax.ShapeDtypeStruct((S, 2048), BF16),
            jax.ShapeDtypeStruct((STEPS, 2048, 128), BF16),
            jax.ShapeDtypeStruct((2048, 128), F32),
            jax.ShapeDtypeStruct((S, 128), F32),
        ),
        in_specs=[SMEM] + [VMEM] * 6,
        out_specs=(VMEM,) * 5,
        compiler_params=params(10),
        name="sort_weights",
        cost_estimate=COST,
    )(info, *ws)


def gather_planes(at, info_ref, *refs):
    pieces, out_ref = refs[:4], refs[4]
    me = info_ref[0]
    for j in range(4):
        rows = pl.ds(pl.multiple_of(((me & 3) ^ j) * SB, SB), SB)
        for p in range(2):
            out_ref[p, rows, :] = pieces[j][SB * (at[j] + p):SB * (at[j] + p + 1)]


def gather_call(info, pieces, at):
    return pl.pallas_call(
        functools.partial(gather_planes, at),
        out_shape=jax.ShapeDtypeStruct((2, S, LN), BF16),
        in_specs=[SMEM] + [VMEM] * 4,
        out_specs=VMEM,
        compiler_params=params(6),
        name="gather_planes",
        cost_estimate=COST,
    )(info, *pieces)


def by_place(info_ref, body):
    for even in (True, False):
        for first in (True, False):
            here = ((info_ref[1] & 1) == (0 if even else 1)) & ((info_ref[0] >> 2) == (0 if first else 1))

            @pl.when(here)
            def _(even=even, first=first):
                body(even, first)


def put_edges(info_ref, place, a, b, ev_ref, od_ref, peer_ref, chip_ref, rows):
    even, first = place
    core = info_ref[0] & 1
    one, two = (a, b) if first else (b, a)
    ev, od = (two[1], one[0]) if even else (one[0], two[1])
    ev_ref[rows, :] = ev.astype(BF16)
    od_ref[rows, :] = od.astype(BF16)
    for q in range(2):
        sides = [(one[q][:, cut].astype(F32), two[q][:, cut].astype(F32)) for cut in (slice(0, 128), slice(LN - 128, LN))]
        low = lax.broadcasted_iota(jnp.int32, sides[0][0].shape, 1) < GY
        left = jnp.where(low, sides[0][0], pltpu.roll(sides[0][1], GY, 1))
        right = jnp.where(low, pltpu.roll(sides[1][0], GY, 1), sides[1][1])
        peer_ref[q, rows, :] = jnp.where(core == 0, right, left).astype(BF16)
        chip_ref[q, rows, :] = jnp.where(core == 0, left, right).astype(BF16)


EDGES = (
    jax.ShapeDtypeStruct((S, LN), BF16),
    jax.ShapeDtypeStruct((S, LN), BF16),
    jax.ShapeDtypeStruct((2, S, 128), BF16),
    jax.ShapeDtypeStruct((2, S, 128), BF16),
)


def gather_far(at, info_ref, a_ref, *refs):
    pieces, out_ref, edges = refs[:4], refs[4], refs[5:]
    gather_planes(at, info_ref, *pieces, out_ref)

    def body(*place):
        def block(s, _):
            rows = pl.ds(pl.multiple_of(s * SB, SB), SB)
            a, b = [[ref[0, rows, :], ref[1, rows, :]] for ref in (a_ref, out_ref)]
            put_edges(info_ref, place, a, b, *edges, rows)
            return 0

        lax.fori_loop(0, S // SB, block, 0, unroll=2)

    by_place(info_ref, body)


def gather_far_call(info, a, pieces, at):
    return pl.pallas_call(
        functools.partial(gather_far, at),
        out_shape=(jax.ShapeDtypeStruct((2, S, LN), BF16),) + EDGES,
        in_specs=[SMEM] + [VMEM] * 5,
        out_specs=(VMEM,) * 5,
        compiler_params=params(6),
        name="gather_far",
        cost_estimate=COST,
    )(info, a, *pieces)


def react(far, conc_ref, cell_ref, order_ref, stoich_ref, load_ref, lr_ref, change_ref, flux_s):
    logs = jnp.log(conc_ref[0].astype(F32)).astype(BF16)
    zeros = jnp.zeros((K, LN), BF16)
    if far:
        hi, lo = cell_ref[...], zeros
    else:
        hi, lo = cell_ref[0, 0, :K], cell_ref[0, 0, K:]
    cells = jnp.concatenate([hi, lo, hi, zeros], axis=0)
    for i in range(N):
        rows = pl.ds(i * 256, 256)
        expo = jnp.dot(order_ref[rows, :], logs, preferred_element_type=F32)
        noise = jnp.dot(load_ref[0, rows, :], cells, preferred_element_type=F32)
        lr = lr_ref[rows, :]
        root = jnp.exp2(expo * HALF_LOG2E + jnp.concatenate([lr] * (LN // 128), axis=1))
        flux_s[rows, :] = (root * (root + noise)).astype(BF16)
    change_ref[0] = jnp.dot(stoich_ref[...], flux_s[...], preferred_element_type=F32)


def react_call(step, conc, cells, sorted_ws, far=False):
    order, stoich, load, lr, _ = sorted_ws
    plane = pl.BlockSpec((1, S, LN), lambda p: (p, 0, 0))
    if far:
        cell = pl.BlockSpec((K, LN), lambda p: (4 * SB // K + 2 * step + p, 0))
    else:
        cell = pl.BlockSpec((1, 1, 2 * K, LN), lambda p: (step, p, 0, 0))
    return pl.pallas_call(
        functools.partial(react, far),
        grid=(2,),
        out_shape=jax.ShapeDtypeStruct((2, S, LN), F32),
        in_specs=[
            plane,
            cell,
            pl.BlockSpec((2048, S), lambda p: (0, 0)),
            pl.BlockSpec((S, 2048), lambda p: (0, 0)),
            pl.BlockSpec((1, 2048, 128), lambda p: (step, 0, 0)),
            pl.BlockSpec((2048, 128), lambda p: (0, 0)),
        ],
        out_specs=plane,
        scratch_shapes=[pltpu.VMEM((2048, LN), BF16)],
        compiler_params=params(20),
        name="react",
        cost_estimate=COST,
    )(conc, cells, order, stoich, load, lr)


def diffuse(info_ref, place, which, a, b, ev, od, from_peer, from_chip, change, coef):
    me = info_ref[0]
    ring = info_ref[1]
    even, first = place[0], place[1] == (which == 0)
    own, other = (a, b) if which == 0 else (b, a)
    own, other = [v.astype(F32) for v in own], [v.astype(F32) for v in other]
    if first:
        lo = jnp.where(ring == 0, own[0], (od if even else ev).astype(F32))
        below, above = [lo, own[0]], [own[1], other[0]]
    else:
        hi = jnp.where(ring == 15, own[1], (ev if even else od).astype(F32))
        below, above = [other[1], own[0]], [own[1], hi]
    rows = own[0].shape[0]
    lane = lax.broadcasted_iota(jnp.int32, (rows, 128), 1)
    low = lane < GY
    column = lane & (GY - 1)
    core = me & 1
    out = []
    for p in range(2):
        c = own[p]
        peer, chip = from_peer[p].astype(F32), from_chip[p].astype(F32)
        left, right = jnp.where(core == 0, chip, peer), jnp.where(core == 0, peer, chip)
        if first:
            right = pltpu.roll(right, GY, 1)
        else:
            left = pltpu.roll(left, GY, 1)
        vs = [c[:, 128 * j:128 * j + 128] for j in range(LN // 128)]
        vb = [v.astype(BF16) for v in vs]
        sw = [pltpu.roll(v, GY, 1).astype(F32) for v in vb]
        left = jnp.where(me == 0, vs[0], left)
        right = jnp.where(me == N - 1, vs[-1], right)
        lat = []
        for j, v in enumerate(vs):
            prev = left if j == 0 else sw[j - 1]
            nxt = right if j == len(vs) - 1 else sw[j + 1]
            x_dn = jnp.where(low, prev, sw[j])
            x_up = jnp.where(low, sw[j], nxt)
            y_up = jnp.where(column == GY - 1, v, pltpu.roll(vb[j], 127, 1).astype(F32))
            y_dn = jnp.where(column == 0, v, pltpu.roll(vb[j], 1, 1).astype(F32))
            lat.append(x_up + x_dn + y_up + y_dn)
        lap = above[p] + below[p] + jnp.concatenate(lat, axis=1) - 6.0 * c
        co = jnp.concatenate([coef] * (LN // 128), axis=1)
        out.append(jnp.maximum(c + co * lap + change[p], FLOOR))
    return out


def two(ref):
    return [ref[0], ref[1]]


ROWS = 32


def near_rows(rows, a_ref, b_ref, ev_ref, od_ref, peer_ref, chip_ref):
    def pair(ref):
        return [ref[0, rows, :], ref[1, rows, :]]

    return pair(a_ref), pair(b_ref), ev_ref[rows, :], od_ref[rows, :], pair(peer_ref), pair(chip_ref)


def advance(info_ref, a_ref, b_ref, da_ref, db_ref, ev_ref, od_ref, peer_ref, chip_ref, coef_ref, na_ref, nb_ref, *edges):
    def body(*place):
        def block(s, _):
            rows = pl.ds(pl.multiple_of(s * ROWS, ROWS), ROWS)
            args = near_rows(rows, a_ref, b_ref, ev_ref, od_ref, peer_ref, chip_ref)
            new = []
            for which, d_ref, out_ref in ((0, da_ref, na_ref), (1, db_ref, nb_ref)):
                change = [d_ref[0, rows, :], d_ref[1, rows, :]]
                new.append(diffuse(info_ref, place, which, *args, change, coef_ref[rows, :]))
                out_ref[0, rows, :], out_ref[1, rows, :] = new[-1]
            put_edges(info_ref, place, *new, *edges, rows)
            return 0

        lax.fori_loop(0, S // ROWS, block, 0, unroll=4)

    by_place(info_ref, body)


def advance_call(info, a, b, da, db, halos, coef):
    pair = jax.ShapeDtypeStruct((2, S, LN), F32)
    return pl.pallas_call(
        advance,
        in_specs=[SMEM] + [VMEM] * 9,
        out_specs=(VMEM,) * 6,
        out_shape=(pair, pair) + EDGES,
        compiler_params=params(16),
        name="advance",
        cost_estimate=COST,
    )(info, a, b, da, db, *halos, coef)


def finish(which, info_ref, a_ref, b_ref, d_ref, ev_ref, od_ref, peer_ref, chip_ref, coef_ref, *outs):
    me = info_ref[0]
    places = [(ref, i) for ref in outs for i in range(ref.shape[0])]

    def body(*place):
        for j, (out, at) in enumerate(places):
            for s in range(SB // ROWS):
                rows = pl.ds(pl.multiple_of(((me & 3) ^ j) * SB + s * ROWS, ROWS), ROWS)
                args = near_rows(rows, a_ref, b_ref, ev_ref, od_ref, peer_ref, chip_ref)
                new = diffuse(info_ref, place, which, *args, [d_ref[0, rows, :], d_ref[1, rows, :]], coef_ref[rows, :])
                for p in range(2):
                    out[at, p, s * ROWS:(s + 1) * ROWS, :] = new[p].astype(BF16)

    by_place(info_ref, body)


def finish_call(which, info, a, b, d, halos, coef, counts):
    return pl.pallas_call(
        functools.partial(finish, which),
        in_specs=[SMEM] + [VMEM] * 8,
        out_specs=(VMEM,) * len(counts),
        out_shape=[jax.ShapeDtypeStruct((n, 2, SB, LN), BF16) for n in counts],
        compiler_params=params(12),
        name="finish",
        cost_estimate=COST,
    )(info, a, b, d, *halos, coef)


def join_out(at, info_ref, *refs):
    pieces, out_ref, buf, sem = refs[:N], refs[N], refs[N + 1], refs[N + 2]
    me = info_ref[0]
    copies = []
    for k in range(N):
        lanes = pl.ds(pl.multiple_of((me ^ k) * LN, LN), LN)
        for p in range(2):
            buf[k, :, p, :] = pieces[k][at[k], p].astype(F32)
        c = pltpu.make_async_copy(buf.at[k], out_ref.at[:, :, lanes], sem.at[k])
        c.start()
        copies.append(c)
    for c in copies:
        c.wait()


def join_call(info, pieces, at):
    return pl.pallas_call(
        functools.partial(join_out, at),
        out_shape=jax.ShapeDtypeStruct((SB, 2, N * LN), F32),
        in_specs=[SMEM] + [VMEM] * N,
        out_specs=pl.BlockSpec(memory_space=pl.ANY),
        scratch_shapes=[pltpu.VMEM((N, SB, 2, LN), F32), pltpu.SemaphoreType.DMA((N,))],
        compiler_params=params(12),
        name="join_out",
        cost_estimate=COST,
    )(info, *pieces)


def send(v, k):
    return lax.ppermute(v, RING, [(i, i ^ k) for i in range(N)])


def swap(v, axis, firsts):
    return lax.ppermute(v, axis, [(i, i + 1) for i in firsts] + [(i + 1, i) for i in firsts])


def exchange(edges):
    ev, od, peer, chip = edges
    od = swap(od, "zy", range(1, 15, 2))
    ev = swap(ev, "zy", range(0, 15, 2))
    return ev, od, send(peer, 1), swap(chip, RING, (1, 3, 5))


def on_device(conc, order, stoich, species_class, diff_coef, rate, noise_load, cell_noise):
    info = jnp.stack([lax.axis_index(RING), lax.axis_index("zy")]).astype(jnp.int32)
    w = weights_call(
        order, stoich, jnp.transpose(noise_load, (0, 2, 1)), rate[None, :], species_class[None, :], diff_coef
    )
    far = lax.ppermute(w, RING, [(i, i ^ (6 if i % 2 else 2)) for i in range(N)])
    beside = send(w, 1)
    after_w, w = lax.optimization_barrier((info, w))
    mine, peer, inner, opp, outer, near = state_call(after_w, conc, cell_noise)
    far, mine = lax.optimization_barrier((far, mine))
    inner, opp, outer = send(inner, 2), send(opp, 4), send(outer, 6)
    ws = sort_call(info, [w, beside, far, *[send(far[:, lo:hi], 1) for lo, hi in zip(PARTS, PARTS[1:])]])
    inner, *ws = lax.optimization_barrier((inner, *ws))
    coef = ws[-1]
    a = gather_call(info, [mine, send(peer, 1), inner, send(inner[2 * SB:], 1)], (0, 0, 0, 0))
    da = react_call(0, a, near, ws)
    opp, outer, da = lax.optimization_barrier((opp, outer, da))
    cells = outer
    b, *edges = gather_far_call(info, a, [opp, send(opp, 1), outer, send(outer, 1)], (0, 2, 0, 2))
    around = exchange(edges)
    db = react_call(0, b, cells, ws, far=True)
    a, b, *edges = advance_call(info, a, b, da, db, around, coef)
    around = exchange(edges)
    db = react_call(1, b, cells, ws, far=True)
    opp, outer = finish_call(1, info, a, b, db, around, coef, (2, 2))
    opp, outer, near = lax.optimization_barrier((opp, outer, near))
    opp, outer = send(opp, 4), send(outer, 6)
    da = react_call(1, a, near, ws)
    mine, peer, inner = finish_call(0, info, a, b, da, around, coef, (1, 1, 2))
    opp, outer, mine = lax.optimization_barrier((opp, outer, mine))
    inner = send(inner, 2)
    back = [mine, send(peer, 1), inner, send(inner[1:], 1), opp, send(opp, 1), outer, send(outer, 1)]
    return join_call(info, back, (0, 0, 0, 0, 0, 1, 0, 1))


def solution(mesh):
    grid = Mesh(mesh.devices.reshape(16, 2, 2, 2), ("zy", "x_hi", "x_lo", "core"))
    rxn, slab = ("x_lo", "core"), ("zy", "x_hi")
    placed = (
        P(rxn, slab, None),
        P(rxn, None),
        P(None, rxn),
        P(rxn),
        P(),
        P(rxn),
        P(None, rxn, None),
        P(None, None, slab, None),
    )
    return jax.shard_map(
        on_device, mesh=grid, in_specs=placed, out_specs=P(rxn, slab, None), check_vma=False
    )
```
